128 devices in a mesh: gx: 8 (over x, core), gy: 16 (over z, y).
Axes of the slice: x: 4, y: 4, z: 4, core: 2. Of those that a mesh axis runs over, the one named last changes fastest.
Arguments:
- density: bfloat16 [64, 1048576], P(None, ('gx', 'gy')), may hold values from -6 to 6
- points: bfloat16 [3, 1048576], P(None, ('gx', 'gy')), may hold values from -4 to 4
- weights: bfloat16 [1048576], P(('gx', 'gy')), may hold values from 0.0099487305 to 0.039794922
- source_basis: bfloat16 [64, 1048576], P(None, ('gx', 'gy')), may hold values from -0.375 to 0.375
- target_basis: bfloat16 [64, 1048576], P(None, ('gx', 'gy')), may hold values from -0.75 to 0.75
- up_transfer: bfloat16 [4096, 4096], P(('gx', 'gy')), may hold values from -0.375 to 0.375
- down_transfer: bfloat16 [4096, 4096], P(('gx', 'gy')), may hold values from -0.75 to 0.75
- couple_leaf: bfloat16 [4096, 8, 4096], P(('gx', 'gy')), may hold values from -0.25 to 0.25
- couple_upper: bfloat16 [1024, 8, 4096], P(('gx', 'gy')), may hold values from -0.25 to 0.25
- owner_leaf: int32 [4096, 8], P(('gx', 'gy')), may hold values from 0 to 127, all different within a row; in each aligned block of 32 rows (0 to 31, 32 to 63, ...) at most 3 rows name the same one
- local_leaf: int32 [4096, 8], P(('gx', 'gy')), may hold values from 0 to 31
- owner_upper: int32 [1024, 8], P(('gx', 'gy')), may hold values from 0 to 127, all different within a row; in each aligned block of 8 rows (0 to 7, 8 to 15, ...) at most 2 rows name the same one
- local_upper: int32 [1024, 8], P(('gx', 'gy')), may hold values from 0 to 7
- near_list: int32 [4096, 9], P(('gx', 'gy')), may hold values from 0 to 4095, as said below
Outputs:
- product: bfloat16 [64, 1048576], P(None, ('gx', 'gy'))
The draws below stay inside these ranges and needn't reach their ends.
Inputs may be any that keep to these rules, and one draw needn't show every extreme that they name: `owner_leaf`: each leaf's row names 8 different devices; among the leaves of one device no device is named more than 3 times, and some device is named exactly 3 times. `owner_upper`: each upper cluster's row names 8 different devices; among the upper clusters of one device no device is named more than 2 times, and some device is named exactly 2 times. `near_list`: entry 0 of each leaf's row is the leaf itself; the other 8 entries are distinct other leaves at most 32 places from it in the cyclic order of leaves, and in every draw some entries lie exactly 32 places away.
All inputs are finite; a program needn't handle non-finite values.
Results may differ from the reference program's by a relative error of at most 0.005.
The reference program's roundings to bfloat16 on the way (of `leaf_mult`, `upper_mult`, `upper_local`, `leaf_local` and `kernel`) count: a program that leaves them out, or rounds other values in their place, can miss the bound.
Values may be sent and summed in bfloat16 or wider, within the bound.
No kernel may reach another device: no remote copies, remote signals or barrier semaphores. Data moves between devices by JAX's collectives and lax.ppermute only.
A program may use at most 128 MiB of HBM per device.

```python
import math
import jax
import jax.numpy as jnp
import numpy as np
from jax import lax

L = 256
R = 64
NRHS = 64
LEAF_DEV = 32
NB = 9
IL0 = 8
IL1 = 8
CL1_DEV = 8
LEAVES = 4096
CLUST1 = 1024
POINTS = 1048576
CAP0 = 3
CAP1 = 2
DEVICES = 128


def draw_near_list(key, part):
    key = jax.random.fold_in(key, 11)
    order_key, place_key, sign_key = jax.random.split(key, 3)
    reach_width = LEAF_DEV
    row_keys = jax.random.split(order_key, LEAVES)
    orders = jax.vmap(lambda row_key: jax.random.permutation(row_key, 2 * reach_width))(row_keys)
    places = jax.random.randint(place_key, (LEAVES // LEAF_DEV,), 0, LEAF_DEV)
    sign_bits = jax.random.randint(sign_key, (LEAVES // LEAF_DEV,), 0, 2)
    leaf_ids = jnp.arange(LEAVES, dtype=jnp.int32)
    forced = leaf_ids % LEAF_DEV == jnp.repeat(places, LEAF_DEV)
    extreme = jnp.repeat(sign_bits, LEAF_DEV) * (2 * reach_width - 1)
    location = jnp.argmax(orders == extreme[:, None], axis=1)
    leading = orders[:, 0]
    columns = jnp.arange(2 * reach_width)[None, :]
    swapped = jnp.where(columns == location[:, None], leading[:, None], orders)
    swapped = swapped.at[:, 0].set(extreme)
    orders = jnp.where(forced[:, None], swapped, orders)
    picked = orders[:, :NB - 1]
    offsets = jnp.where(picked < reach_width, picked - reach_width, picked - reach_width + 1)
    others = (leaf_ids[:, None] + offsets) % LEAVES
    return jnp.concatenate([leaf_ids[:, None], others], axis=1).astype(jnp.int32)


def set_ends(drawn, rng, low, top_value):
    place = [jax.random.randint(jax.random.fold_in(rng, axis), (), 0, length) for axis, length in enumerate(drawn.shape)]
    main_axis = drawn.shape.index(max(drawn.shape))
    neighbour = place[:main_axis] + [(place[main_axis] + 1) % drawn.shape[main_axis]] + place[main_axis + 1:]
    return drawn.at[tuple(place)].set(low).at[tuple(neighbour)].set(top_value)


def block_levels(rng, extent, shards, least, high):
    def one(axis_at, shards_of):
        steps = jax.random.uniform(jax.random.fold_in(jax.random.fold_in(rng, 6), axis_at), (shards_of,), jnp.float32, least / len(shards), high / len(shards))
        return jnp.repeat(jnp.exp(steps), extent[axis_at] // shards_of).reshape((-1,) + (1,) * (len(extent) - axis_at - 1))

    loudness = one(*shards[0])
    for cut in shards[1:]:
        loudness = loudness * one(*cut)
    return loudness


def deal_out(rng, own, number, rows, amount, top, limit, slope):
    sequence = jax.random.permutation(rng, amount)
    crowded, usual = portions_of(amount, rows * top, limit, slope, True), portions_of(amount, rows * top, limit, slope, False)
    places = jnp.arange(amount)

    def named(lengths, rotation):
        used = int((lengths > 0).sum())
        fixed = max(1, used // 4)
        moved = fixed + (places - fixed + rotation * (used - fixed)) % max(1, amount - fixed)
        return jnp.zeros((amount,), jnp.int32).at[sequence[jnp.where(places < fixed, places, moved)]].set(jnp.asarray(lengths, jnp.int32))

    lengths = jnp.where(number % 4 == 0, named(crowded, number // 4), named(usual, number - number // 4 - 1))
    mixed = jax.random.permutation(jax.random.fold_in(own, 3), amount)
    donor, sink = mixed[0:amount // 2 * 2:2], mixed[1:amount // 2 * 2:2]
    slack = jnp.minimum(lengths[donor] - 1, limit - lengths[sink]) // 2
    slack = jnp.where((donor == sequence[0]) | (sink == sequence[0]) | (lengths[sink] == 0), 0, jnp.maximum(slack, 0))
    moved = jax.random.randint(jax.random.fold_in(own, 4), (amount // 2,), 0, 1 << 20) % (slack + 1)
    lengths = lengths.at[donor].add(-moved).at[sink].add(moved)
    labels = jnp.searchsorted(jnp.cumsum(lengths), jnp.arange(rows * top), side="right").astype(jnp.int32)
    grid = labels.reshape(top, rows).T
    grid = grid[jax.random.permutation(jax.random.fold_in(own, 1), rows)]
    rotation = jax.random.randint(jax.random.fold_in(own, 2), (rows, 1), 0, top)
    return jnp.take_along_axis(grid, (jnp.arange(top)[None, :] + rotation) % top, axis=1)


def portions_of(number_of, total, limit, lean, full):
    weights = [(1 << 20) // math.isqrt(grade ** lean) + 1 for grade in range(1, number_of + 1)]
    largest = limit if full else min(limit, max(-(-total // number_of), total * weights[0] // sum(weights)))
    least = 1 if total - largest >= number_of - 1 else 0
    holding, surplus = [largest] + [least] * (number_of - 1), total - largest - least * (number_of - 1)
    while surplus > 0:
        movable = [i for i in range(1, number_of) if holding[i] < largest] or [i for i in range(1, number_of) if holding[i] < limit]
        mass, left = sum([weights[i] for i in movable]), surplus
        for i in movable:
            extra = min(limit - holding[i], max(1, left * weights[i] // mass), surplus)
            holding[i] = holding[i] + extra
            surplus = surplus - extra
    return np.array(holding)


def scatter_about(own_key, shape, scale, most, cuts=(), kind=jnp.bfloat16):
    entries = jax.random.normal(own_key, shape, jnp.float32) * scale
    if len(cuts) > 0:
        entries = block_levels(own_key, shape, cuts, -0.22, 0.18) * entries
    return jnp.clip(entries, min=-most, max=most).astype(kind)


def setup_inputs(seed: int = 0) -> dict:
    keys = jax.random.split(jax.random.key(seed), 15)
    density = scatter_about(keys[0], (NRHS, POINTS), 1.0, 6.0, ((1, 128),))
    points = scatter_about(keys[1], (3, POINTS), 1.0, 4.0, ((1, 128),))
    weights = jnp.clip(jnp.exp(math.log(0.039794922) - 1.3862944 * jax.random.uniform(keys[2], (POINTS,), jnp.float32) ** block_levels(keys[2], (POINTS,), ((0, 128),), -0.2, 0.2)), 0.0099487305, 0.039794922).astype(jnp.bfloat16)
    source_basis = scatter_about(keys[3], (R, POINTS), L ** -0.5, 0.375, ((1, 128),))
    target_basis = scatter_about(keys[4], (R, POINTS), R ** -0.5, 0.75, ((1, 128),))
    up_transfer = scatter_about(keys[5], (LEAVES, R * R), (4 * R) ** -0.5, 0.375, ((0, 128),))
    down_transfer = scatter_about(keys[6], (LEAVES, R * R), R ** -0.5, 0.75, ((0, 128),))
    couple_leaf = scatter_about(keys[7], (LEAVES, IL0, R * R), (R * IL0) ** -0.5, 0.25, ((0, 128),))
    couple_upper = scatter_about(keys[8], (CLUST1, IL1, R * R), (R * IL1) ** -0.5, 0.25, ((0, 128),))
    owner_leaf_keys = jax.random.split(jax.random.fold_in(keys[9], 1), LEAVES // LEAF_DEV)
    owner_leaf_turns = jax.random.permutation(jax.random.fold_in(keys[9], 3), LEAVES // LEAF_DEV)
    owner_leaf = jax.vmap(lambda own, number: deal_out(jax.random.fold_in(keys[9], 2), own, number, LEAF_DEV, DEVICES, IL0, CAP0, 2))(owner_leaf_keys, owner_leaf_turns).reshape((LEAVES, IL0))
    local_leaf = set_ends(jax.random.randint(keys[10], (LEAVES, IL0), 0, LEAF_DEV), jax.random.fold_in(keys[10], 1), 0, LEAF_DEV - 1).astype(jnp.int32)
    owner_upper_keys = jax.random.split(jax.random.fold_in(keys[11], 1), CLUST1 // CL1_DEV)
    owner_upper_turns = jax.random.permutation(jax.random.fold_in(keys[11], 3), CLUST1 // CL1_DEV)
    owner_upper = jax.vmap(lambda own, number: deal_out(jax.random.fold_in(keys[11], 2), own, number, CL1_DEV, DEVICES, IL1, CAP1, 2))(owner_upper_keys, owner_upper_turns).reshape((CLUST1, IL1))
    local_upper = set_ends(jax.random.randint(keys[12], (CLUST1, IL1), 0, CL1_DEV), jax.random.fold_in(keys[12], 1), 0, CL1_DEV - 1).astype(jnp.int32)
    near_list = draw_near_list(jax.random.fold_in(keys[14], 71), 0)
    return {"density": density, "points": points, "weights": weights, "source_basis": source_basis, "target_basis": target_basis, "up_transfer": up_transfer, "down_transfer": down_transfer, "couple_leaf": couple_leaf, "couple_upper": couple_upper, "owner_leaf": owner_leaf, "local_leaf": local_leaf, "owner_upper": owner_upper, "local_upper": local_upper, "near_list": near_list}


SOFTEN = 0.0025

def near_kernel(target_points, source_points, source_weights):
    target_points = target_points.astype(jnp.float32)
    source_points = source_points.astype(jnp.float32)
    first_diff = target_points[0][:, None, :, None] - source_points[0][:, :, None, :]
    second_diff = target_points[1][:, None, :, None] - source_points[1][:, :, None, :]
    third_diff = target_points[2][:, None, :, None] - source_points[2][:, :, None, :]
    distance = first_diff * first_diff + second_diff * second_diff + third_diff * third_diff
    scaled = source_weights.astype(jnp.float32)[:, :, None, :] * lax.rsqrt(distance + SOFTEN)
    return scaled.astype(jnp.bfloat16)

def couple(multipoles, owner, local, matrices, per_dev):
    blocks = LEAVES // LEAF_DEV
    source_ids = (owner * per_dev + local).astype(jnp.int32)
    id_blocks = source_ids.reshape(blocks, per_dev, source_ids.shape[1])
    matrix_blocks = matrices.reshape(blocks, per_dev, matrices.shape[1], R, R)

    def one_block(block_pair):
        block_ids, block_matrices = block_pair
        gathered = jnp.take(multipoles, block_ids, axis=0).astype(jnp.float32)
        return jnp.einsum('cknr,ckrs->cns', gathered, block_matrices.astype(jnp.float32))
    return lax.map(one_block, (id_blocks, matrix_blocks)).reshape(blocks * per_dev, NRHS, R)

def reference(density, points, weights, source_basis, target_basis, up_transfer, down_transfer, couple_leaf, couple_upper, owner_leaf, local_leaf, owner_upper, local_upper, near_list):
    density_cube = density.reshape(NRHS, LEAVES, L)
    leaf_mult = jnp.einsum('ncp,rcp->cnr', density_cube.astype(jnp.float32), source_basis.reshape(R, LEAVES, L).astype(jnp.float32)).astype(jnp.bfloat16)
    children = leaf_mult.reshape(CLUST1, 4, NRHS, R).astype(jnp.float32)
    up_mats = up_transfer.reshape(CLUST1, 4, R, R).astype(jnp.float32)
    upper_mult = jnp.einsum('jcnr,jcrs->jns', children, up_mats).astype(jnp.bfloat16)
    upper_local = couple(upper_mult, owner_upper, local_upper, couple_upper, CL1_DEV).astype(jnp.bfloat16)
    down_mats = down_transfer.reshape(CLUST1, 4, R, R).astype(jnp.float32)
    handed = jnp.einsum('jns,jcsr->jcnr', upper_local.astype(jnp.float32), down_mats).reshape(LEAVES, NRHS, R)
    leaf_local = (couple(leaf_mult, owner_leaf, local_leaf, couple_leaf, LEAF_DEV) + handed).astype(jnp.bfloat16)
    far_field = jnp.einsum('cnr,rcp->ncp', leaf_local.astype(jnp.float32), target_basis.reshape(R, LEAVES, L).astype(jnp.float32))
    point_cube = points.reshape(3, LEAVES, L)
    weight_rows = weights.reshape(LEAVES, L)

    def near_block(first_row):
        source_ids = lax.dynamic_slice_in_dim(near_list, first_row, LEAF_DEV, 0)
        target_points = lax.dynamic_slice_in_dim(point_cube, first_row, LEAF_DEV, 1)
        kernel = near_kernel(target_points, jnp.take(point_cube, source_ids, axis=1), jnp.take(weight_rows, source_ids, axis=0))
        source_density = jnp.take(density_cube, source_ids, axis=1).astype(jnp.float32)
        return jnp.einsum('gkpq,ngkq->ngp', kernel.astype(jnp.float32), source_density)
    first_rows = jnp.arange(LEAVES // LEAF_DEV, dtype=jnp.int32) * LEAF_DEV
    near_parts = lax.map(near_block, first_rows)
    near_field = near_parts.transpose(1, 0, 2, 3).reshape(NRHS, LEAVES, L)
    return (far_field + near_field).reshape(NRHS, POINTS).astype(jnp.bfloat16)
```

```python
import jax
import jax.numpy as jnp
from jax import lax
from jax.experimental import pallas as pl
from jax.experimental.pallas import tpu as pltpu
from jax.sharding import PartitionSpec as P

SOFTEN = 0.0025
AXES = ("gx", "gy")
CAP_LEAF = 3
CAP_UPPER = 2
SLOTS = CAP_LEAF + CAP_UPPER
F32 = jnp.float32
BF16 = jnp.bfloat16
NN = (((1,), (0,)), ((), ()))
NT = (((1,), (1,)), ((), ()))
TN = (((0,), (0,)), ((), ()))
VMEM = pl.BlockSpec(memory_space=pltpu.VMEM)
SMEM = pl.BlockSpec(memory_space=pltpu.SMEM)


def dot(a, b, dims=NN):
    return lax.dot_general(a, b, dims, preferred_element_type=F32)


def passed_along(value, steps):
    count = lax.axis_size(AXES)
    pairs = [(source, (source + steps) % count) for source in range(count)]
    return lax.ppermute(value, AXES, pairs)


def iota(shape, dim):
    return lax.broadcasted_iota(jnp.int32, shape, dim)


def flat_row(table):
    rows, wide = table.shape
    spread = (iota((wide, rows * wide), 1) % wide == iota((wide, rows * wide), 0)).astype(BF16)
    keep = iota((rows, rows * wide), 1) // wide == iota((rows, rows * wide), 0)
    return jnp.sum(
        jnp.where(keep, dot(table.astype(F32).astype(BF16), spread), 0.0), axis=0, keepdims=True
    )


def slots_of(owner, local, first, cap, devices, shift):
    entries = owner.shape[1]
    hit = owner == iota((devices, entries), 0).astype(F32)
    ones = hit.astype(BF16)
    before = (iota((entries, entries), 0) < iota((entries, entries), 1)).astype(BF16)
    rank = jnp.sum(jnp.where(hit, dot(ones, before), 0.0), axis=0, keepdims=True)
    wanted = jnp.where(
        rank + first == iota((8, entries), 0).astype(F32), local + shift, 0.0
    ).astype(BF16)
    return dot(ones, wanted, NT), owner * SLOTS + first + rank


def request_kernel(own_leaf, loc_leaf, own_upper, loc_upper, req_ref, leaf_ref, upper_ref):
    devices = req_ref.shape[0]
    leaf_dev = own_leaf.shape[0]
    req_leaf, at_leaf = slots_of(
        flat_row(own_leaf[...]), flat_row(loc_leaf[...]), 0, CAP_LEAF, devices, 0
    )
    req_upper, at_upper = slots_of(
        flat_row(own_upper[...]), flat_row(loc_upper[...]), CAP_LEAF, CAP_UPPER, devices, leaf_dev
    )
    req_ref[...] = (req_leaf + req_upper).astype(jnp.int32)
    leaf_ref[...] = at_leaf.astype(jnp.int32)
    upper_ref[...] = at_upper.astype(jnp.int32)


def packed(block):
    half = block.shape[0] // 2
    return jnp.concatenate([block[:half], block[half:]], axis=1).astype(BF16)


def multipole_kernel(density, basis, up_ref, table_ref):
    leaf_dev = up_ref.shape[0] // up_ref.shape[1]
    rank = up_ref.shape[1]
    size = density.shape[1] // leaf_dev
    for upper in range(leaf_dev // 4):
        blocks = []
        for leaf in range(4 * upper, 4 * upper + 4):
            cut = slice(leaf * size, (leaf + 1) * size)
            blocks.append(dot(basis[:, cut], density[:, cut], NT).astype(BF16))
            table_ref[leaf] = packed(blocks[-1].astype(F32))
        mats = up_ref[4 * upper * rank : 4 * (upper + 1) * rank]
        total = dot(mats, jnp.concatenate(blocks, axis=0), TN)
        table_ref[leaf_dev + upper] = packed(total)


def serve_kernel(req, table_ref, out_ref):
    per_step = out_ref.shape[0]
    first = pl.program_id(0) * per_step
    half = table_ref.shape[1]
    for t in range(per_step):
        for slot in range(SLOTS):
            row = req[(first + t) * 8 + slot]
            out_ref[t, slot * half : (slot + 1) * half] = table_ref[row]


def pieces(value):
    high = value.astype(BF16).astype(F32)
    middle = (value - high).astype(BF16).astype(F32)
    return high, middle, value - high - middle


def near_kernel(offsets, before, own, following, out_ref, window, scale, rhs, lhs, kern):
    leaves, rows, size = out_ref.shape
    near = offsets.shape[0] // leaves
    one = jnp.ones((3, size), F32)
    zero = jnp.zeros((7, size), F32)
    for place, ref in enumerate((before, own, following)):

        def fill(i, carry, place=place, ref=ref):
            block = ref[:, pl.ds(pl.multiple_of(i * size, size), size)]
            window[place * leaves + i] = block[:rows]
            y = block[rows:].astype(F32)
            scale[place * leaves + i] = y[3:4]
            square = y[0:1] * y[0:1] + y[1:2] * y[1:2] + y[2:3] * y[2:3]
            rhs[place * leaves + i] = jnp.concatenate(
                [-2.0 * y[0:3], one, *pieces(square + SOFTEN), zero], axis=0
            ).astype(BF16)
            if place == 1:
                lhs[i] = jnp.transpose(
                    jnp.concatenate([y[0:3], *pieces(square), one, zero], axis=0)
                ).astype(BF16)
            return carry

        lax.fori_loop(0, leaves, fill, 0)

    def leaf(c, carry):
        for k in range(near):
            w = offsets[c * near + k]
            square = dot(lhs[c], rhs[w])
            kern[k] = (scale[w] * lax.rsqrt(square)).astype(BF16)
        total = jnp.zeros((rows, size), F32)
        for k in range(near):
            total += dot(window[offsets[c * near + k]], kern[k], NT)
        out_ref[c] = total
        return carry

    lax.fori_loop(0, leaves, leaf, 0)


def near_field(offsets, before, own, following, leaves, rows):
    size = own.shape[1] // leaves
    near = offsets.shape[0] // leaves
    return pl.pallas_call(
        near_kernel,
        out_shape=jax.ShapeDtypeStruct((leaves, rows, size), F32),
        in_specs=[SMEM, VMEM, VMEM, VMEM],
        out_specs=VMEM,
        scratch_shapes=[
            pltpu.VMEM((3 * leaves, rows, size), BF16),
            pltpu.VMEM((3 * leaves, 1, size), F32),
            pltpu.VMEM((3 * leaves, 16, size), BF16),
            pltpu.VMEM((leaves, size, 16), BF16),
            pltpu.VMEM((near, size, size), BF16),
        ],
        compiler_params=pltpu.CompilerParams(vmem_limit_bytes=40 << 20),
        cost_estimate=pl.CostEstimate(
            flops=20 * leaves * near * size * size * rows,
            bytes_accessed=6 << 20,
            transcendentals=leaves * near * size * size,
        ),
        name="near",
    )(offsets, before, own, following)


def folded(pair, rank):
    return pair[:rank, :rank] + pair[rank:, rank:]


def final_kernel(at_leaf, at_upper, replies, upper_mats, leaf_mats, down, basis, near, out_ref):
    step = pl.program_id(0)
    rank = down.shape[2]
    vectors, wide = out_ref.shape
    size = wide // 4
    fan = upper_mats.shape[2] // (rank // 2)

    def gathered(places, first):
        return jnp.concatenate([replies[places[first + k]] for k in range(fan)], axis=0)

    upper = folded(dot(upper_mats[0], gathered(at_upper, step * fan)), rank).astype(BF16)
    handed = dot(down[0], upper)
    for child in range(4):
        pair = dot(leaf_mats[child], gathered(at_leaf, (step * 4 + child) * fan))
        local = folded(pair, rank) + handed[child * rank : (child + 1) * rank]
        far = dot(local.astype(BF16), basis[:, child * size : (child + 1) * size], TN)
        out_ref[:, child * size : (child + 1) * size] = (far + near[child]).astype(BF16)


def coupled(mats, rank):
    count, fan = mats.shape[:2]
    cut = mats.reshape(count, fan, 2, rank // 2, rank)
    return cut.transpose(0, 2, 4, 1, 3).reshape(count, 2 * rank, fan * rank // 2)


def body(
    density,
    points,
    weights,
    source_basis,
    target_basis,
    up_transfer,
    down_transfer,
    couple_leaf,
    couple_upper,
    owner_leaf,
    local_leaf,
    owner_upper,
    local_upper,
    near_list,
):
    devices = lax.axis_size(AXES)
    leaves, fan = owner_leaf.shape
    uppers = owner_upper.shape[0]
    vectors = density.shape[0]
    rank = source_basis.shape[0]
    half = rank // 2
    size = density.shape[1] // leaves
    total_leaves = leaves * devices

    requests, at_leaf, at_upper = pl.pallas_call(
        request_kernel,
        out_shape=(
            jax.ShapeDtypeStruct((devices, 8), jnp.int32),
            jax.ShapeDtypeStruct((1, leaves * fan), jnp.int32),
            jax.ShapeDtypeStruct((1, uppers * fan), jnp.int32),
        ),
        in_specs=[VMEM] * 4,
        out_specs=(VMEM, VMEM, VMEM),
        name="requests",
    )(owner_leaf, local_leaf, owner_upper, local_upper)
    asked = lax.all_to_all(requests, AXES, split_axis=0, concat_axis=0, tiled=True)

    own = jnp.concatenate(
        [density, points, weights[None], jnp.zeros((4, density.shape[1]), BF16)], axis=0
    )
    before = passed_along(own, 1)
    following = passed_along(own, -1)

    table = pl.pallas_call(
        multipole_kernel,
        out_shape=jax.ShapeDtypeStruct((leaves + uppers, half, 2 * rank), BF16),
        in_specs=[VMEM] * 3,
        out_specs=VMEM,
        name="multipoles",
    )(density, source_basis, up_transfer.reshape(leaves * rank, rank))

    per_step = 16
    found = pl.pallas_call(
        serve_kernel,
        out_shape=jax.ShapeDtypeStruct((devices, SLOTS * half, 2 * rank), BF16),
        grid_spec=pltpu.PrefetchScalarGridSpec(
            num_scalar_prefetch=1,
            grid=(devices // per_step,),
            in_specs=[pl.BlockSpec(table.shape, lambda i, r: (0, 0, 0))],
            out_specs=pl.BlockSpec((per_step, SLOTS * half, 2 * rank), lambda i, r: (i, 0, 0)),
        ),
        name="serve",
    )(asked.reshape(-1), table)
    replies = lax.all_to_all(found, AXES, split_axis=0, concat_axis=0, tiled=True)

    offsets = (near_list - lax.axis_index(AXES) * leaves + leaves) % total_leaves
    near = near_field(offsets.reshape(-1), before, own, following, leaves, vectors)

    leaf_mats = coupled(couple_leaf, rank)
    upper_mats = coupled(couple_upper, rank)
    down = (
        down_transfer.reshape(uppers, 4, rank, rank)
        .transpose(0, 1, 3, 2)
        .reshape(uppers, 4 * rank, rank)
    )
    whole = (devices * SLOTS, half, 2 * rank)
    return pl.pallas_call(
        final_kernel,
        out_shape=jax.ShapeDtypeStruct(density.shape, BF16),
        grid_spec=pltpu.PrefetchScalarGridSpec(
            num_scalar_prefetch=2,
            grid=(uppers,),
            in_specs=[
                pl.BlockSpec(whole, lambda i, a, b: (0, 0, 0)),
                pl.BlockSpec((1, 2 * rank, fan * half), lambda i, a, b: (i, 0, 0)),
                pl.BlockSpec((4, 2 * rank, fan * half), lambda i, a, b: (i, 0, 0)),
                pl.BlockSpec((1, 4 * rank, rank), lambda i, a, b: (i, 0, 0)),
                pl.BlockSpec((rank, 4 * size), lambda i, a, b: (0, i)),
                pl.BlockSpec((4, vectors, size), lambda i, a, b: (i, 0, 0)),
            ],
            out_specs=pl.BlockSpec((vectors, 4 * size), lambda i, a, b: (0, i)),
        ),
        compiler_params=pltpu.CompilerParams(vmem_limit_bytes=40 << 20),
        name="far",
    )(
        at_leaf.reshape(-1),
        at_upper.reshape(-1),
        replies.reshape(whole),
        upper_mats,
        leaf_mats,
        down,
        target_basis,
        near,
    )


def solution(mesh):
    whole = AXES
    placed = (
        P(None, whole),
        P(None, whole),
        P(whole),
        P(None, whole),
        P(None, whole),
        P(whole, None),
        P(whole, None),
        P(whole, None, None),
        P(whole, None, None),
        P(whole, None),
        P(whole, None),
        P(whole, None),
        P(whole, None),
        P(whole, None),
    )
    return jax.shard_map(
        body, mesh=mesh, in_specs=placed, out_specs=P(None, whole), check_vma=False
    )
```

```python
import jax
import jax.numpy as jnp
from jax import lax
from jax.experimental import pallas as pl
from jax.experimental.pallas import tpu as pltpu
from jax.sharding import PartitionSpec as P

SOFTEN = 0.0025
AXES = ("gx", "gy")
SENT = 56
MOST = 80
F32 = jnp.float32
BF16 = jnp.bfloat16
NN = (((1,), (0,)), ((), ()))
NT = (((1,), (1,)), ((), ()))
TN = (((0,), (0,)), ((), ()))
VMEM = pl.BlockSpec(memory_space=pltpu.VMEM)
SMEM = pl.BlockSpec(memory_space=pltpu.SMEM)


def dot(a, b, dims=NN):
    return lax.dot_general(a, b, dims, preferred_element_type=F32)


def passed_along(value, steps):
    count = lax.axis_size(AXES)
    pairs = [(source, (source + steps) % count) for source in range(count)]
    return lax.ppermute(value, AXES, pairs)


def iota(shape, dim):
    return lax.broadcasted_iota(jnp.int32, shape, dim)


def folded(pair, rank):
    return pair[:rank, :rank] + pair[rank:, rank:]


def flat_row(table):
    wide, rows = table.shape
    spread = (iota((rows, rows * wide), 1) // wide == iota((rows, rows * wide), 0)).astype(BF16)
    keep = iota((wide, rows * wide), 1) % wide == iota((wide, rows * wide), 0)
    return jnp.sum(
        jnp.where(keep, dot(table.astype(F32).astype(BF16), spread), 0.0), axis=0, keepdims=True
    ).astype(jnp.int32)


def request_kernel(own_leaf, loc_leaf, own_upper, loc_upper, ask_ref, place_ref):
    groups = ask_ref.shape[0]
    members = place_ref.shape[0]
    leaves = own_leaf.shape[1]
    owner = jnp.concatenate([flat_row(own_leaf[...]), flat_row(own_upper[...])], axis=1)
    row = jnp.concatenate([flat_row(loc_leaf[...]), flat_row(loc_upper[...]) + leaves], axis=1)
    entries = owner.shape[1]
    group = owner // members
    member = owner - group * members
    hit = group == iota((groups, entries), 0)
    ones = hit.astype(BF16)
    before = (iota((entries, entries), 0) < iota((entries, entries), 1)).astype(BF16)
    rank = jnp.sum(jnp.where(hit, dot(ones, before), 0.0), axis=0, keepdims=True).astype(jnp.int32)
    here = rank == iota((128, entries), 0)
    wanted = [
        dot(ones, jnp.where(here, part.astype(F32), 0.0).astype(BF16), NT) for part in (member, row)
    ]
    most = jnp.max(jnp.sum(hit.astype(F32), axis=1, keepdims=True), axis=0, keepdims=True)
    wanted[0] = jnp.where(iota((groups, 128), 1) == 127, most, wanted[0])
    both = jnp.concatenate(wanted, axis=1)
    for g in range(groups):
        ask_ref[g] = jnp.broadcast_to(both[g : g + 1], ask_ref.shape[1:]).astype(BF16)
    place_ref[...] = jnp.where(iota(place_ref.shape, 0) == 0, group, rank)


def multipole_kernel(density, basis, up_ref, out_ref, square, table, up):
    leaves = up_ref.shape[0]
    rank = square.shape[1]
    half = rank // 2
    rows = table.shape[0] // half
    size = density.shape[1] // leaves
    for leaf in range(leaves):
        cut = slice(leaf * size, (leaf + 1) * size)
        square[leaf * rank : (leaf + 1) * rank] = dot(basis[:, cut], density[:, cut], NT)

    def pack(first, count):
        even = square[pl.ds(first * rank, count * half, stride=2)]
        odd = square[pl.ds(first * rank + 1, count * half, stride=2)]
        table[first * half : (first + count) * half] = jnp.concatenate([even, odd], axis=1)

    pack(0, leaves)
    for j in range(half):
        up[pl.ds(j, leaves, stride=half)] = up_ref[:, j * 2 * rank : (j + 1) * 2 * rank].astype(F32)
    for upper in range(rows - leaves):
        cut = slice(upper * 4 * half, (upper + 1) * 4 * half)
        pair = dot(up[cut].astype(BF16), table[cut].astype(BF16), TN)
        square[(leaves + upper) * rank : (leaves + upper + 1) * rank] = folded(pair, rank)
    pack(leaves, rows - leaves)
    for j in range(half):
        out_ref[j // 2, :, (j % 2) * 2 * rank : (j % 2 + 1) * 2 * rank] = table[
            pl.ds(j, rows, stride=half)
        ].astype(BF16)


def serve_kernel(first, slices, out_ref, codes):
    step = pl.program_id(0)
    members, count, wide = slices.shape
    rows = out_ref.shape[1]
    groups = codes.shape[0]

    @pl.when(step == 0)
    def _():
        asked = slices[:, count - groups :, :].astype(F32)
        code = asked[:, :, : wide // 2] * count + asked[:, :, wide // 2 :]
        for g in range(groups):
            codes[g] = jnp.transpose(code[:, g])

    column = codes[step, first : first + rows]
    lanes = iota((rows, members * count), 1).astype(F32)
    picks = jnp.concatenate(
        [jnp.where(column[:, t : t + 1] == lanes, 1.0, 0.0) for t in range(members)], axis=0
    ).astype(BF16)
    found = dot(picks, slices[...].reshape(members * count, wide))
    out_ref[...] = found.reshape(members, rows, wide).astype(BF16)


def serve(slices, groups, first, rows):
    members, count, wide = slices.shape
    return pl.pallas_call(
        lambda *refs: serve_kernel(first, *refs),
        out_shape=jax.ShapeDtypeStruct((groups * members, rows, wide), BF16),
        grid=(groups,),
        in_specs=[pl.BlockSpec(slices.shape, lambda i: (0, 0, 0))],
        out_specs=pl.BlockSpec((members, rows, wide), lambda i: (i, 0, 0)),
        scratch_shapes=[pltpu.VMEM((groups, wide // 2, members), F32)],
        compiler_params=pltpu.CompilerParams(vmem_limit_bytes=24 << 20),
        name="serve",
    )(slices)


def select_kernel(stride, place_ref, out_ref):
    place = place_ref[0:1] * stride + place_ref[1:2]
    column = jnp.transpose(jnp.broadcast_to(place.astype(F32), (8, place.shape[1])))[:, 0:1]
    out_ref[...] = jnp.where(column == iota(out_ref.shape, 1).astype(F32), 1.0, 0.0).astype(BF16)


def select(places, entries, groups, stride):
    return pl.pallas_call(
        lambda *refs: select_kernel(stride, *refs),
        out_shape=jax.ShapeDtypeStruct((entries, groups * stride), BF16),
        in_specs=[VMEM],
        out_specs=VMEM,
        name="select",
    )(places)


def arrange_kernel(couple, out_ref):
    for c in range(couple.shape[0]):
        mats = couple[c].astype(F32)
        tall = jnp.concatenate(
            [mats[:, j * 128 : (j + 1) * 128] for j in range(mats.shape[1] // 128)], axis=0
        )
        out_ref[c] = jnp.transpose(tall).astype(BF16)


def arrange(couple):
    count, fan, wide = couple.shape
    per_step = 8
    return pl.pallas_call(
        arrange_kernel,
        out_shape=jax.ShapeDtypeStruct((count, 128, wide * fan // 128), BF16),
        grid=(count // per_step,),
        in_specs=[pl.BlockSpec((per_step, fan, wide), lambda i: (i, 0, 0))],
        out_specs=pl.BlockSpec((per_step, 128, wide * fan // 128), lambda i: (i, 0, 0)),
        name="arrange",
    )(couple)


def pieces(value):
    high = value.astype(BF16).astype(F32)
    middle = (value - high).astype(BF16).astype(F32)
    return high, middle, value - high - middle


def near_kernel(offsets, before, own, following, out_ref, window, scale, rhs, lhs, kern):
    leaves, rows, size = out_ref.shape
    near = offsets.shape[0] // leaves
    one = jnp.ones((3, size), F32)
    zero = jnp.zeros((7, size), F32)
    for place, ref in enumerate((before, own, following)):

        def fill(i, carry, place=place, ref=ref):
            block = ref[:, pl.ds(pl.multiple_of(i * size, size), size)]
            window[place * leaves + i] = block[:rows]
            y = block[rows:].astype(F32)
            scale[place * leaves + i] = y[3:4]
            square = y[0:1] * y[0:1] + y[1:2] * y[1:2] + y[2:3] * y[2:3]
            rhs[place * leaves + i] = jnp.concatenate(
                [-2.0 * y[0:3], one, *pieces(square + SOFTEN), zero], axis=0
            ).astype(BF16)
            if place == 1:
                lhs[i] = jnp.transpose(
                    jnp.concatenate([y[0:3], *pieces(square), one, zero], axis=0)
                ).astype(BF16)
            return carry

        lax.fori_loop(0, leaves, fill, 0)

    def leaf(c, carry):
        for k in range(near):
            w = offsets[c * near + k]
            square = dot(lhs[c], rhs[w])
            kern[k] = (scale[w] * lax.rsqrt(square)).astype(BF16)
        total = jnp.zeros((rows, size), F32)
        for k in range(near):
            total += dot(window[offsets[c * near + k]], kern[k], NT)
        out_ref[c] = total
        return carry

    lax.fori_loop(0, leaves, leaf, 0)


def near_field(offsets, before, own, following, leaves, rows):
    size = own.shape[1] // leaves
    near = offsets.shape[0] // leaves
    return pl.pallas_call(
        near_kernel,
        out_shape=jax.ShapeDtypeStruct((leaves, rows, size), F32),
        in_specs=[SMEM, VMEM, VMEM, VMEM],
        out_specs=VMEM,
        scratch_shapes=[
            pltpu.VMEM((3 * leaves, rows, size), BF16),
            pltpu.VMEM((3 * leaves, 1, size), F32),
            pltpu.VMEM((3 * leaves, 16, size), BF16),
            pltpu.VMEM((leaves, size, 16), BF16),
            pltpu.VMEM((near, size, size), BF16),
        ],
        compiler_params=pltpu.CompilerParams(vmem_limit_bytes=40 << 20),
        cost_estimate=pl.CostEstimate(
            flops=20 * leaves * near * size * size * rows,
            bytes_accessed=6 << 20,
            transcendentals=leaves * near * size * size,
        ),
        name="near",
    )(offsets, before, own, following)


def final_kernel(counts, *refs):
    replies, refs = refs[: len(counts)], refs[len(counts) :]
    chosen, upper_mats, leaf_mats, down, basis, near, out_ref, taken, held, handed = refs
    uppers, leaves = upper_mats.shape[0], leaf_mats.shape[0]
    rank = down.shape[2]
    size = basis.shape[1] // leaves
    groups = handed.shape[0]
    members = replies[0].shape[0] // groups
    stride = taken.shape[1] // groups
    fan = chosen.shape[0] // (uppers + leaves)
    taken[...] = jnp.zeros(taken.shape, BF16)
    for m in range(members):
        first = 0
        for reply, count in zip(replies, counts):
            for g in range(groups):
                taken[m % 2, g * stride + first : g * stride + first + count] = reply[
                    g * members + m
                ]
            first += count
        block = dot(chosen[...], taken[m % 2]).reshape(uppers + leaves, fan, 2 * 2 * rank)
        held[:, m * 2 * fan : (m + 1) * 2 * fan] = jnp.concatenate(
            [block[:, :, : 2 * rank], block[:, :, 2 * rank :]], axis=1
        ).astype(BF16)
    for j in range(uppers):
        upper = folded(dot(upper_mats[j], held[leaves + j]), rank).astype(BF16)
        handed[j] = dot(down[j], upper)
    for c in range(leaves):
        cut = slice(c * size, (c + 1) * size)
        local = folded(dot(leaf_mats[c], held[c]), rank)
        local += handed[c // 4, c % 4 * rank : (c % 4 + 1) * rank]
        far = dot(local.astype(BF16), basis[:, cut], TN)
        out_ref[:, cut] = (far + near[c]).astype(BF16)


def final(replies, chosen, groups, upper_mats, leaf_mats, down, basis, near, shape):
    uppers, rank = down.shape[0], down.shape[2]
    counts = [reply.shape[1] for reply in replies]
    wide = upper_mats.shape[2]
    return pl.pallas_call(
        lambda *refs: final_kernel(counts, *refs),
        out_shape=jax.ShapeDtypeStruct(shape, BF16),
        in_specs=[VMEM] * (len(replies) + 6),
        out_specs=VMEM,
        scratch_shapes=[
            pltpu.VMEM((2, chosen.shape[1], replies[0].shape[2]), BF16),
            pltpu.VMEM((uppers + leaf_mats.shape[0], wide, 2 * rank), BF16),
            pltpu.VMEM((uppers, 4 * rank, rank), F32),
        ],
        compiler_params=pltpu.CompilerParams(vmem_limit_bytes=32 << 20),
        name="far",
    )(*replies, chosen, upper_mats, leaf_mats, down, basis, near)


def exchange(value, axes):
    return lax.all_to_all(value, axes, split_axis=0, concat_axis=0, tiled=True)


def body(
    density,
    points,
    weights,
    source_basis,
    target_basis,
    up_transfer,
    down_transfer,
    couple_leaf,
    couple_upper,
    owner_leaf,
    local_leaf,
    owner_upper,
    local_upper,
    near_list,
):
    devices = lax.axis_size(AXES)
    groups, members = lax.axis_size("gx"), lax.axis_size("gy")
    leaves, fan = owner_leaf.shape
    uppers = owner_upper.shape[0]
    vectors = density.shape[0]
    rank = source_basis.shape[0]
    half = rank // 2
    rows = leaves + uppers

    own = jnp.concatenate(
        [density, points, weights[None], jnp.zeros((4, density.shape[1]), BF16)], axis=0
    )
    before = passed_along(own, 1)
    following = passed_along(own, -1)

    asks, places = pl.pallas_call(
        request_kernel,
        out_shape=(
            jax.ShapeDtypeStruct((groups, 16, 256), BF16),
            jax.ShapeDtypeStruct((members, rows * fan), jnp.int32),
        ),
        in_specs=[VMEM] * 4,
        out_specs=(VMEM, VMEM),
        name="requests",
    )(owner_leaf.T, local_leaf.T, owner_upper.T, local_upper.T)
    asked = exchange(asks, "gx")

    slices = pl.pallas_call(
        multipole_kernel,
        out_shape=jax.ShapeDtypeStruct((members, rows, 4 * rank), BF16),
        in_specs=[VMEM] * 3,
        out_specs=VMEM,
        scratch_shapes=[
            pltpu.VMEM((rows * rank, vectors), F32),
            pltpu.VMEM((rows * half, 2 * vectors), F32),
            pltpu.VMEM((leaves * half, 2 * rank), F32),
        ],
        compiler_params=pltpu.CompilerParams(vmem_limit_bytes=16 << 20),
        name="multipoles",
    )(density, source_basis, up_transfer)
    asked = jnp.broadcast_to(asked[None, :, 0, :], (members, groups, asked.shape[2]))
    slices = exchange(jnp.concatenate([slices, asked], axis=1), "gy")

    leaf_mats = arrange(couple_leaf)
    upper_mats = arrange(couple_upper)
    slices, before, following, leaf_mats, upper_mats = lax.optimization_barrier(
        (slices, before, following, leaf_mats, upper_mats)
    )
    replies = exchange(serve(slices, groups, 0, SENT), AXES)

    offsets = (near_list - lax.axis_index(AXES) * leaves + leaves) % (leaves * devices)
    near = near_field(offsets.reshape(-1), before, own, following, leaves, vectors)
    down = (
        down_transfer.reshape(uppers, 4, rank, rank)
        .transpose(0, 1, 3, 2)
        .reshape(uppers, 4 * rank, rank)
    )
    chosen = select(places, rows * fan, groups, 64)

    def finish(received, picks):
        return final(
            received, picks, groups, upper_mats, leaf_mats, down, target_basis, near, density.shape
        )

    def some_left():
        others = exchange(serve(slices, groups, SENT, MOST - SENT), AXES)
        return finish((replies, others), select(places, rows * fan, groups, MOST))

    most = jnp.max(slices[:, rows:, 127].astype(F32))
    return lax.cond(most > SENT, some_left, lambda: finish((replies,), chosen))


def solution(mesh):
    whole = AXES
    placed = (
        P(None, whole),
        P(None, whole),
        P(whole),
        P(None, whole),
        P(None, whole),
        P(whole, None),
        P(whole, None),
        P(whole, None, None),
        P(whole, None, None),
        P(whole, None),
        P(whole, None),
        P(whole, None),
        P(whole, None),
        P(whole, None),
    )
    return jax.shard_map(
        body, mesh=mesh, in_specs=placed, out_specs=P(None, whole), check_vma=False
    )
```

```python
import jax
import jax.numpy as jnp
from jax import lax
from jax.experimental import pallas as pl
from jax.experimental.pallas import tpu as pltpu
from jax.sharding import PartitionSpec as P

SOFTEN = 0.0025
AXES = ("gx", "gy")
SENT = 28
MOST = 40
F32 = jnp.float32
BF16 = jnp.bfloat16
NN = (((1,), (0,)), ((), ()))
NT = (((1,), (1,)), ((), ()))
TN = (((0,), (0,)), ((), ()))
VMEM = pl.BlockSpec(memory_space=pltpu.VMEM)
ANY = pl.BlockSpec(memory_space=pl.ANY)
ROOM = 60 << 20
SMEM = pl.BlockSpec(memory_space=pltpu.SMEM)


def dot(a, b, dims=NN):
    return lax.dot_general(a, b, dims, preferred_element_type=F32)


def passed_along(value, steps):
    count = lax.axis_size(AXES)
    pairs = [(source, (source + steps) % count) for source in range(count)]
    return lax.ppermute(value, AXES, pairs)


def iota(shape, dim):
    return lax.broadcasted_iota(jnp.int32, shape, dim)


def folded(pair, rank):
    return pair[:rank, :rank] + pair[rank:, rank:]


def flat_row(table):
    wide, rows = table.shape
    spread = (iota((rows, rows * wide), 1) // wide == iota((rows, rows * wide), 0)).astype(BF16)
    keep = iota((wide, rows * wide), 1) % wide == iota((wide, rows * wide), 0)
    return jnp.sum(
        jnp.where(keep, dot(table.astype(F32).astype(BF16), spread), 0.0), axis=0, keepdims=True
    ).astype(jnp.int32)


def request_kernel(own_leaf, loc_leaf, own_upper, loc_upper, ask_ref, place_ref):
    groups = ask_ref.shape[0]
    leaves, uppers = own_leaf.shape[1], own_upper.shape[0]
    tall_owner, tall_row = jnp.transpose(own_upper[...]), jnp.transpose(loc_upper[...])
    owner = jnp.concatenate([flat_row(own_leaf[...]), flat_row(tall_owner)], axis=1)
    row = jnp.concatenate([flat_row(loc_leaf[...]), flat_row(tall_row) + leaves], axis=1)
    entries = owner.shape[1]
    member = owner // groups
    group = owner - member * groups
    hit = group == iota((groups, entries), 0)
    ones = hit.astype(BF16)
    before = (iota((entries, entries), 0) < iota((entries, entries), 1)).astype(BF16)
    rank = jnp.sum(jnp.where(hit, dot(ones, before), 0.0), axis=0, keepdims=True).astype(jnp.int32)
    slot = jnp.where(rank < SENT, rank, rank + SENT)
    second = slot + jnp.where(rank < SENT, SENT, MOST - SENT)
    first_here = slot == iota((128, entries), 0)
    second_here = second == iota((128, entries), 0)
    far_row = row + (leaves + uppers)
    members = jnp.where(first_here | second_here, member, 0)
    rows = jnp.where(first_here, row, jnp.where(second_here, far_row, 0))
    wanted = [dot(ones, part.astype(F32).astype(BF16), NT) for part in (members, rows)]
    most = jnp.max(jnp.sum(hit.astype(F32), axis=1, keepdims=True), axis=0, keepdims=True)
    wanted[0] = jnp.where(iota((groups, 128), 1) == 127, most, wanted[0])
    both = jnp.concatenate(wanted, axis=1)
    for g in range(groups):
        ask_ref[g] = jnp.broadcast_to(both[g : g + 1], ask_ref.shape[1:]).astype(BF16)
    place_ref[...] = jnp.where(iota(place_ref.shape, 0) == 0, group, rank)


def multipole_kernel(density, basis, up_ref, out_ref, square, table, up):
    leaves = up_ref.shape[0]
    rank = square.shape[1]
    half = rank // 2
    rows = table.shape[0] // half
    size = density.shape[1] // leaves
    for leaf in range(leaves):
        cut = slice(leaf * size, (leaf + 1) * size)
        square[leaf * rank : (leaf + 1) * rank] = dot(basis[:, cut], density[:, cut], NT)

    def pack(first, count):
        even = square[pl.ds(first * rank, count * half, stride=2)]
        odd = square[pl.ds(first * rank + 1, count * half, stride=2)]
        table[first * half : (first + count) * half] = jnp.concatenate([even, odd], axis=1)

    pack(0, leaves)
    for j in range(half):
        up[pl.ds(j, leaves, stride=half)] = up_ref[:, j * 2 * rank : (j + 1) * 2 * rank].astype(F32)
    for upper in range(rows - leaves):
        cut = slice(upper * 4 * half, (upper + 1) * 4 * half)
        pair = dot(up[cut].astype(BF16), table[cut].astype(BF16), TN)
        square[(leaves + upper) * rank : (leaves + upper + 1) * rank] = folded(pair, rank)
    pack(leaves, rows - leaves)
    for m in range(out_ref.shape[0]):
        parts = [table[pl.ds(4 * m + a, rows, stride=half)] for a in range(4)]
        pairs = [jnp.concatenate(parts[:2], axis=1), jnp.concatenate(parts[2:], axis=1)]
        out_ref[m] = jnp.concatenate(pairs, axis=0).astype(BF16)


def serve_kernel(first, slices, out_ref, codes):
    step = pl.program_id(0)
    members, count, wide = slices.shape
    rows = out_ref.shape[1]
    asking = codes.shape[2]
    some = out_ref.shape[0] // asking

    @pl.when(step == 0)
    def _():
        asked = slices[:, count - asking :, :].astype(F32)
        code = asked[:, :, : wide // 2] * count + asked[:, :, wide // 2 :]
        for m in range(members):
            codes[m] = jnp.transpose(code[m])

    lanes = iota((rows, members * count), 1).astype(F32)
    table = slices[...].reshape(members * count, wide)
    for m in range(some):
        column = codes[step * some + m, first : first + rows]
        for t in range(0, asking, 4):
            picks = jnp.concatenate(
                [jnp.where(column[:, u : u + 1] == lanes, 1.0, 0.0) for u in range(t, t + 4)],
                axis=0,
            ).astype(BF16)
            out_ref[m * asking + t : m * asking + t + 4] = (
                dot(picks, table).reshape(4, rows, wide).astype(BF16)
            )


def serve(slices, asking, first, rows):
    members, count, wide = slices.shape
    some = members // 2
    return pl.pallas_call(
        lambda *refs: serve_kernel(first, *refs),
        out_shape=jax.ShapeDtypeStruct((members * asking, rows, wide), BF16),
        grid=(members // some,),
        in_specs=[pl.BlockSpec(slices.shape, lambda i: (0, 0, 0))],
        out_specs=pl.BlockSpec((some * asking, rows, wide), lambda i: (i, 0, 0)),
        scratch_shapes=[pltpu.VMEM((members, wide // 2, asking), F32)],
        compiler_params=pltpu.CompilerParams(vmem_limit_bytes=ROOM),
        name="serve",
    )(slices)


def arrange_kernel(couple, out_ref):
    for c in range(couple.shape[0]):
        mats = couple[c].astype(F32)
        tall = jnp.concatenate(
            [mats[:, j * 128 : (j + 1) * 128] for j in range(mats.shape[1] // 128)], axis=0
        )
        out_ref[c] = jnp.transpose(tall).astype(BF16)


def arrange(couple):
    count, fan, wide = couple.shape
    per_step = 8
    return pl.pallas_call(
        arrange_kernel,
        out_shape=jax.ShapeDtypeStruct((count, 128, wide * fan // 128), BF16),
        grid=(count // per_step,),
        in_specs=[pl.BlockSpec((per_step, fan, wide), lambda i: (i, 0, 0))],
        out_specs=pl.BlockSpec((per_step, 128, wide * fan // 128), lambda i: (i, 0, 0)),
        compiler_params=pltpu.CompilerParams(vmem_limit_bytes=ROOM),
        name="arrange",
    )(couple)


def pieces(value):
    high = value.astype(BF16).astype(F32)
    middle = (value - high).astype(BF16).astype(F32)
    return high, middle, value - high - middle


def near_kernel(listed, first, before, own, following, out_ref, window, sources, targets, kern):
    leaves, rows, size = out_ref.shape
    near = listed.shape[0]
    wide = own.shape[1]
    total = first[1]
    one = jnp.ones((3, wide), F32)
    zero = jnp.zeros((6, wide), F32)
    for place, ref in enumerate((before, own, following)):
        cut = slice(place * wide, (place + 1) * wide)
        window[:, cut] = ref[:rows]
        y = ref[rows:].astype(F32)
        square = y[0:1] * y[0:1] + y[1:2] * y[1:2] + y[2:3] * y[2:3]
        sources[cut] = jnp.transpose(
            jnp.concatenate([-2.0 * y[0:3], one, *pieces(square + SOFTEN), y[3:4], zero], axis=0)
        ).astype(BF16)
        if place == 1:
            targets[...] = jnp.concatenate(
                [y[0:3], *pieces(square), one, zero, zero[:1]], axis=0
            ).astype(BF16)

    def span(leaf):
        return pl.ds(pl.multiple_of(leaf * size, size), size)

    def place_of(c, k):
        offset = listed[k, c] - first[0] + leaves
        offset = jnp.where(offset < 0, offset + total, offset)
        return span(jnp.where(offset >= total, offset - total, offset))

    def fill(c, k, slot):
        block = sources[place_of(c, k)]
        square = dot(block, targets[:, span(c)])
        kern[slot, k] = (block[:, 9:10].astype(F32) * lax.rsqrt(square)).astype(BF16)

    def both(filled, used, slot):
        sum_ = jnp.zeros((rows, size), F32)
        for k in range(near):
            fill(filled, k, 1 - slot)
            sum_ += dot(window[:, place_of(used, k)], kern[slot, k])
        out_ref[used] = sum_

    for k in range(near):
        fill(0, k, 0)

    def two(i, carry):
        both(2 * i + 1, 2 * i, 0)
        both(jnp.minimum(2 * i + 2, leaves - 1), 2 * i + 1, 1)
        return carry

    lax.fori_loop(0, leaves // 2, two, 0)


def near_field(listed, first, before, own, following, leaves, rows):
    wide = own.shape[1]
    size = wide // leaves
    near = listed.shape[0]
    return pl.pallas_call(
        near_kernel,
        out_shape=jax.ShapeDtypeStruct((leaves, rows, size), F32),
        in_specs=[SMEM, SMEM, VMEM, VMEM, VMEM],
        out_specs=VMEM,
        scratch_shapes=[
            pltpu.VMEM((rows, 3 * wide), BF16),
            pltpu.VMEM((3 * wide, 16), BF16),
            pltpu.VMEM((16, wide), BF16),
            pltpu.VMEM((2, near, size, size), BF16),
        ],
        compiler_params=pltpu.CompilerParams(vmem_limit_bytes=ROOM),
        cost_estimate=pl.CostEstimate(
            flops=400 * leaves * near * size * size * rows,
            bytes_accessed=6 << 20,
            transcendentals=leaves * near * size * size,
        ),
        name="near",
    )(listed, first, before, own, following)


def final_kernel(groups, places, *refs):
    count = (len(refs) - 5) // 2
    sources, out_ref, refs = refs[: count - 1], refs[count - 1], refs[count:]
    targets, out_here, (taken, held, handed, sems, out_sems) = (
        refs[: count - 1],
        refs[count - 1],
        refs[count:],
    )
    replies = targets[:-5]
    upper_mats, down, leaf_mats, basis, near = targets[-5:]
    uppers, leaves = upper_mats.shape[0], leaf_mats.shape[0]
    entries, rank = places.shape[1], down.shape[2]
    members = replies[0].shape[0] // groups
    size = basis.shape[1] // leaves
    fan = entries // (uppers + leaves)
    parts = out_sems.shape[0]
    loads = [
        pltpu.make_async_copy(source, target, sems.at[i])
        for i, (source, target) in enumerate(zip(sources, targets))
    ]
    for load in loads:
        load.start()
    group = jnp.transpose(places[...].astype(F32))
    group, position = group[:, 0:1], group[:, 1:2]
    first = 0
    for number, reply in enumerate(replies):
        rows = reply.shape[1] // 2
        stride = (rows + 15) // 16 * 16
        lane = iota((entries, groups * stride), 1).astype(F32)
        inside = (position >= first) & (position < first + rows)
        wanted = jnp.where(inside, group * stride + position - first, -1.0)
        chosen = jnp.where(wanted == lane, 1.0, 0.0).astype(BF16)
        first += rows
        taken[...] = jnp.zeros(taken.shape, BF16)
        loads[number].wait()
        for m in range(2 * members):
            for g in range(groups):
                taken[m % 2, g * stride : g * stride + rows] = reply[
                    m // 2 * groups + g, m % 2 * rows : (m % 2 + 1) * rows
                ]
            block = dot(chosen, taken[m % 2, : groups * stride])
            block = block.reshape(uppers + leaves, fan, 4 * rank)
            block = jnp.concatenate([block[:, :, : 2 * rank], block[:, :, 2 * rank :]], axis=1)
            cut = slice(m * 2 * fan, (m + 1) * 2 * fan)
            if number == 0:
                held[:, cut] = block.astype(BF16)
            else:
                held[:, cut] += block.astype(BF16)
    loads = loads[len(replies) :]
    loads[0].wait()
    loads[1].wait()
    for j in range(uppers):
        upper = folded(dot(upper_mats[j], held[leaves + j]), rank).astype(BF16)
        handed[j] = dot(down[j], upper)
    loads[2].wait()
    locals_ = []
    for c in range(leaves):
        local = folded(dot(leaf_mats[c], held[c]), rank)
        locals_.append(local + handed[c // 4, c % 4 * rank : (c % 4 + 1) * rank])
    tall = jnp.transpose(jnp.concatenate(locals_, axis=0)).astype(BF16)
    loads[3].wait()
    loads[4].wait()
    stores = []
    for part in range(parts):
        begin = part * leaves // parts
        for c in range(begin, begin + leaves // parts):
            cut = slice(c * size, (c + 1) * size)
            far = dot(tall[:, c * rank : (c + 1) * rank], basis[:, cut])
            out_here[:, cut] = (far + near[c]).astype(BF16)
        cut = pl.ds(begin * size, leaves * size // parts)
        stores.append(
            pltpu.make_async_copy(out_here.at[:, cut], out_ref.at[:, cut], out_sems.at[part])
        )
        stores[-1].start()
    for store in stores:
        store.wait()


def final(groups, places, replies, upper_mats, down, leaf_mats, basis, near):
    uppers, rank = down.shape[0], down.shape[2]
    operands = (*replies, upper_mats, down, leaf_mats, basis, near)
    out = jax.ShapeDtypeStruct((near.shape[1], basis.shape[1]), BF16)
    parts = 4
    return pl.pallas_call(
        lambda *refs: final_kernel(groups, *refs),
        out_shape=out,
        in_specs=[VMEM] + [ANY] * len(operands),
        out_specs=ANY,
        scratch_shapes=[pltpu.VMEM(x.shape, x.dtype) for x in (*operands, out)]
        + [
            pltpu.VMEM((2, groups * 32, replies[0].shape[2]), BF16),
            pltpu.VMEM((uppers + leaf_mats.shape[0], upper_mats.shape[2], 2 * rank), BF16),
            pltpu.VMEM((uppers, 4 * rank, rank), F32),
            pltpu.SemaphoreType.DMA((len(operands),)),
            pltpu.SemaphoreType.DMA((parts,)),
        ],
        compiler_params=pltpu.CompilerParams(vmem_limit_bytes=ROOM),
        name="far",
    )(places, *operands)


def exchange(value, axes):
    return lax.all_to_all(value, axes, split_axis=0, concat_axis=0, tiled=True)


def body(
    density,
    points,
    weights,
    source_basis,
    target_basis,
    up_transfer,
    down_transfer,
    couple_leaf,
    couple_upper,
    owner_leaf,
    local_leaf,
    owner_upper,
    local_upper,
    near_list,
):
    devices = lax.axis_size(AXES)
    members, groups = lax.axis_size("gx"), lax.axis_size("gy")
    leaves, fan = owner_leaf.shape
    uppers = owner_upper.shape[0]
    vectors = density.shape[0]
    rank = source_basis.shape[0]
    half = rank // 2
    rows = leaves + uppers

    asks, places = pl.pallas_call(
        request_kernel,
        out_shape=(
            jax.ShapeDtypeStruct((groups, 16, 256), BF16),
            jax.ShapeDtypeStruct((8, rows * fan), jnp.int32),
        ),
        in_specs=[VMEM] * 4,
        out_specs=(VMEM, VMEM),
        name="requests",
    )(owner_leaf.T, local_leaf.T, owner_upper, local_upper)
    asked = exchange(asks, "gy")
    slices = pl.pallas_call(
        multipole_kernel,
        out_shape=jax.ShapeDtypeStruct((members, 2 * rows, 4 * rank), BF16),
        in_specs=[VMEM] * 3,
        out_specs=VMEM,
        scratch_shapes=[
            pltpu.VMEM((rows * rank, vectors), F32),
            pltpu.VMEM((rows * half, 2 * vectors), F32),
            pltpu.VMEM((leaves * half, 2 * rank), F32),
        ],
        compiler_params=pltpu.CompilerParams(vmem_limit_bytes=ROOM),
        name="multipoles",
    )(density, source_basis, up_transfer)

    slices, asked, density, points, weights = lax.optimization_barrier(
        (slices, asked, density, points, weights)
    )
    own = jnp.concatenate(
        [density, points, weights[None], jnp.zeros((4, density.shape[1]), BF16)], axis=0
    )
    before = passed_along(own, 1)
    following = passed_along(own, -1)
    asked = jnp.broadcast_to(asked[None, :, 0, :], (members, groups, asked.shape[2]))
    slices = jnp.concatenate([slices, asked], axis=1)

    slices, own, couple_leaf, couple_upper, down_transfer = lax.optimization_barrier(
        (slices, own, couple_leaf, couple_upper, down_transfer)
    )
    slices = exchange(slices, "gx")
    upper_mats = arrange(couple_upper)
    leaf_mats = arrange(couple_leaf)
    down = (
        down_transfer.reshape(uppers, 4, rank, rank)
        .transpose(0, 1, 3, 2)
        .reshape(uppers, 4 * rank, rank)
    )
    first = jnp.stack([lax.axis_index(AXES) * leaves, jnp.int32(leaves * devices)])
    slices, leaf_mats, upper_mats, down, first = lax.optimization_barrier(
        (slices, leaf_mats, upper_mats, down, first)
    )
    replies = exchange(serve(slices, groups, 0, 2 * SENT), AXES)
    near = near_field(near_list.T, first, before, own, following, leaves, vectors)
    most = jnp.max(slices[:, 2 * rows :, 127].astype(F32))

    def finish(*received):
        return final(groups, places, received, upper_mats, down, leaf_mats, target_basis, near)

    def some_left():
        others = exchange(serve(slices, groups, 2 * SENT, 2 * (MOST - SENT)), AXES)
        return finish(replies, others)

    return lax.cond(most > SENT, some_left, lambda: finish(replies))


def solution(mesh):
    whole = AXES
    placed = (
        P(None, whole),
        P(None, whole),
        P(whole),
        P(None, whole),
        P(None, whole),
        P(whole, None),
        P(whole, None),
        P(whole, None, None),
        P(whole, None, None),
        P(whole, None),
        P(whole, None),
        P(whole, None),
        P(whole, None),
        P(whole, None),
    )
    return jax.shard_map(
        body, mesh=mesh, in_specs=placed, out_specs=P(None, whole), check_vma=False
    )
```

```python
import jax
import jax.numpy as jnp
from jax import lax
from jax.experimental import pallas as pl
from jax.experimental.pallas import tpu as pltpu
from jax.sharding import PartitionSpec as P

SOFTEN = 0.0025
AXES = ("gx", "gy")
SENT = 28
MOST = 40
F32 = jnp.float32
BF16 = jnp.bfloat16
NN = (((1,), (0,)), ((), ()))
NT = (((1,), (1,)), ((), ()))
TN = (((0,), (0,)), ((), ()))
VMEM = pl.BlockSpec(memory_space=pltpu.VMEM)
ANY = pl.BlockSpec(memory_space=pl.ANY)
ROOM = 60 << 20
SMEM = pl.BlockSpec(memory_space=pltpu.SMEM)


def dot(a, b, dims=NN):
    return lax.dot_general(a, b, dims, preferred_element_type=F32)


def swapped(value, first):
    count = lax.axis_size(AXES)
    pairs = [(one, (one + 1) % count) for one in range(first, count, 2)]
    return lax.ppermute(value, AXES, pairs + [(b, a) for a, b in pairs])


def iota(shape, dim):
    return lax.broadcasted_iota(jnp.int32, shape, dim)


def folded(pair, rank):
    return pair[:rank, :rank] + pair[rank:, rank:]


def flat_row(table):
    wide, rows = table.shape
    spread = (iota((rows, rows * wide), 1) // wide == iota((rows, rows * wide), 0)).astype(BF16)
    keep = iota((wide, rows * wide), 1) % wide == iota((wide, rows * wide), 0)
    return jnp.sum(
        jnp.where(keep, dot(table.astype(F32).astype(BF16), spread), 0.0), axis=0, keepdims=True
    ).astype(jnp.int32)


def request_kernel(own_leaf, loc_leaf, own_upper, loc_upper, ask_ref, place_ref):
    groups = ask_ref.shape[0]
    leaves, uppers = own_leaf.shape[1], own_upper.shape[0]
    tall_owner, tall_row = jnp.transpose(own_upper[...]), jnp.transpose(loc_upper[...])
    owner = jnp.concatenate([flat_row(own_leaf[...]), flat_row(tall_owner)], axis=1)
    row = jnp.concatenate([flat_row(loc_leaf[...]), flat_row(tall_row) + leaves], axis=1)
    entries = owner.shape[1]
    member = owner // groups
    group = owner - member * groups
    hit = group == iota((groups, entries), 0)
    ones = hit.astype(BF16)
    before = (iota((entries, entries), 0) < iota((entries, entries), 1)).astype(BF16)
    rank = jnp.sum(jnp.where(hit, dot(ones, before), 0.0), axis=0, keepdims=True).astype(jnp.int32)
    slot = jnp.where(rank < SENT, rank, rank + SENT)
    second = slot + jnp.where(rank < SENT, SENT, MOST - SENT)
    first_here = slot == iota((128, entries), 0)
    second_here = second == iota((128, entries), 0)
    far_row = row + (leaves + uppers)
    members = jnp.where(first_here | second_here, member, 0)
    rows = jnp.where(first_here, row, jnp.where(second_here, far_row, 0))
    wanted = [dot(ones, part.astype(F32).astype(BF16), NT) for part in (members, rows)]
    most = jnp.max(jnp.sum(hit.astype(F32), axis=1, keepdims=True), axis=0, keepdims=True)
    wanted[0] = jnp.where(iota((groups, 128), 1) == 127, most, wanted[0])
    both = jnp.concatenate(wanted, axis=1)
    for g in range(groups):
        ask_ref[g] = jnp.broadcast_to(both[g : g + 1], ask_ref.shape[1:]).astype(BF16)
    place_ref[...] = jnp.where(iota(place_ref.shape, 0) == 0, group, rank)


def multipole_kernel(density, basis, up_ref, out_ref, square, table, up):
    leaves = up_ref.shape[0]
    rank = square.shape[1]
    half = rank // 2
    rows = table.shape[0] // half
    size = density.shape[1] // leaves
    for leaf in range(leaves):
        cut = slice(leaf * size, (leaf + 1) * size)
        square[leaf * rank : (leaf + 1) * rank] = dot(basis[:, cut], density[:, cut], NT)

    def pack(first, count):
        even = square[pl.ds(first * rank, count * half, stride=2)]
        odd = square[pl.ds(first * rank + 1, count * half, stride=2)]
        table[first * half : (first + count) * half] = jnp.concatenate([even, odd], axis=1)

    pack(0, leaves)
    for j in range(half):
        up[pl.ds(j, leaves, stride=half)] = up_ref[:, j * 2 * rank : (j + 1) * 2 * rank].astype(F32)
    for upper in range(rows - leaves):
        cut = slice(upper * 4 * half, (upper + 1) * 4 * half)
        pair = dot(up[cut].astype(BF16), table[cut].astype(BF16), TN)
        square[(leaves + upper) * rank : (leaves + upper + 1) * rank] = folded(pair, rank)
    pack(leaves, rows - leaves)
    for m in range(out_ref.shape[0]):
        parts = [table[pl.ds(4 * m + a, rows, stride=half)] for a in range(4)]
        pairs = [jnp.concatenate(parts[:2], axis=1), jnp.concatenate(parts[2:], axis=1)]
        out_ref[m] = jnp.concatenate(pairs, axis=0).astype(BF16)


def serve_kernel(first, slices, out_ref, codes):
    step = pl.program_id(0)
    members, count, wide = slices.shape
    rows = out_ref.shape[1]
    asking = codes.shape[2]
    some = out_ref.shape[0] // asking

    @pl.when(step == 0)
    def _():
        asked = slices[:, count - asking :, :].astype(F32)
        code = asked[:, :, : wide // 2] * count + asked[:, :, wide // 2 :]
        for m in range(members):
            codes[m] = jnp.transpose(code[m])

    lanes = iota((rows, members * count), 1).astype(F32)
    table = slices[...].reshape(members * count, wide)
    for m in range(some):
        column = codes[step * some + m, first : first + rows]
        for t in range(0, asking, 4):
            picks = jnp.concatenate(
                [jnp.where(column[:, u : u + 1] == lanes, 1.0, 0.0) for u in range(t, t + 4)],
                axis=0,
            ).astype(BF16)
            out_ref[m * asking + t : m * asking + t + 4] = (
                dot(picks, table).reshape(4, rows, wide).astype(BF16)
            )


def serve(slices, asking, first, rows):
    members, count, wide = slices.shape
    some = members // 2
    return pl.pallas_call(
        lambda *refs: serve_kernel(first, *refs),
        out_shape=jax.ShapeDtypeStruct((members * asking, rows, wide), BF16),
        grid=(members // some,),
        in_specs=[pl.BlockSpec(slices.shape, lambda i: (0, 0, 0))],
        out_specs=pl.BlockSpec((some * asking, rows, wide), lambda i: (i, 0, 0)),
        scratch_shapes=[pltpu.VMEM((members, wide // 2, asking), F32)],
        compiler_params=pltpu.CompilerParams(vmem_limit_bytes=ROOM),
        name="serve",
    )(slices)


def arrange_kernel(couple, out_ref):
    for c in range(couple.shape[0]):
        mats = couple[c].astype(F32)
        tall = jnp.concatenate(
            [mats[:, j * 128 : (j + 1) * 128] for j in range(mats.shape[1] // 128)], axis=0
        )
        out_ref[c] = jnp.transpose(tall).astype(BF16)


def arrange(couple):
    count, fan, wide = couple.shape
    per_step = 8
    return pl.pallas_call(
        arrange_kernel,
        out_shape=jax.ShapeDtypeStruct((count, 128, wide * fan // 128), BF16),
        grid=(count // per_step,),
        in_specs=[pl.BlockSpec((per_step, fan, wide), lambda i: (i, 0, 0))],
        out_specs=pl.BlockSpec((per_step, 128, wide * fan // 128), lambda i: (i, 0, 0)),
        compiler_params=pltpu.CompilerParams(vmem_limit_bytes=ROOM),
        name="arrange",
    )(couple)


def pieces(value):
    high = value.astype(BF16).astype(F32)
    middle = (value - high).astype(BF16).astype(F32)
    return high, middle, value - high - middle


def near_kernel(listed, first, one_side, own, other_side, out_ref, window, sources, targets, kern):
    leaves, rows, size = out_ref.shape
    near = listed.shape[0]
    wide = own.shape[1]
    total = first[1]
    one = jnp.ones((3, wide), F32)
    zero = jnp.zeros((6, wide), F32)
    odd = first[2]
    for ref, place in ((one_side, 2 - 2 * odd), (own, 1), (other_side, 2 * odd)):
        cut = pl.ds(pl.multiple_of(place * wide, wide), wide)
        window[:, cut] = ref[:rows]
        y = ref[rows:].astype(F32)
        square = y[0:1] * y[0:1] + y[1:2] * y[1:2] + y[2:3] * y[2:3]
        sources[cut] = jnp.transpose(
            jnp.concatenate([-2.0 * y[0:3], one, *pieces(square + SOFTEN), y[3:4], zero], axis=0)
        ).astype(BF16)
        if ref is own:
            targets[...] = jnp.concatenate(
                [y[0:3], *pieces(square), one, zero, zero[:1]], axis=0
            ).astype(BF16)

    def span(leaf):
        return pl.ds(pl.multiple_of(leaf * size, size), size)

    def place_of(c, k):
        offset = listed[k, c] - first[0] + leaves
        offset = jnp.where(offset < 0, offset + total, offset)
        return span(jnp.where(offset >= total, offset - total, offset))

    def fill(c, k, slot):
        block = sources[place_of(c, k)]
        square = dot(block, targets[:, span(c)])
        kern[slot, k] = (block[:, 9:10].astype(F32) * lax.rsqrt(square)).astype(BF16)

    def both(filled, used, slot):
        sum_ = jnp.zeros((rows, size), F32)
        for k in range(near):
            fill(filled, k, 1 - slot)
            sum_ += dot(window[:, place_of(used, k)], kern[slot, k])
        out_ref[used] = sum_

    for k in range(near):
        fill(0, k, 0)

    def two(i, carry):
        both(2 * i + 1, 2 * i, 0)
        both(jnp.minimum(2 * i + 2, leaves - 1), 2 * i + 1, 1)
        return carry

    lax.fori_loop(0, leaves // 2, two, 0)


def near_field(listed, first, one_side, own, other_side, leaves, rows):
    wide = own.shape[1]
    size = wide // leaves
    near = listed.shape[0]
    return pl.pallas_call(
        near_kernel,
        out_shape=jax.ShapeDtypeStruct((leaves, rows, size), F32),
        in_specs=[SMEM, SMEM, VMEM, VMEM, VMEM],
        out_specs=VMEM,
        scratch_shapes=[
            pltpu.VMEM((rows, 3 * wide), BF16),
            pltpu.VMEM((3 * wide, 16), BF16),
            pltpu.VMEM((16, wide), BF16),
            pltpu.VMEM((2, near, size, size), BF16),
        ],
        compiler_params=pltpu.CompilerParams(vmem_limit_bytes=ROOM),
        cost_estimate=pl.CostEstimate(
            flops=400 * leaves * near * size * size * rows,
            bytes_accessed=6 << 20,
            transcendentals=leaves * near * size * size,
        ),
        name="near",
    )(listed, first, one_side, own, other_side)


def final_kernel(groups, places, *refs):
    count = (len(refs) - 5) // 2
    sources, out_ref, refs = refs[: count - 1], refs[count - 1], refs[count:]
    targets, out_here, (taken, held, handed, sems, out_sems) = (
        refs[: count - 1],
        refs[count - 1],
        refs[count:],
    )
    replies = targets[:-5]
    upper_mats, down, leaf_mats, basis, near = targets[-5:]
    uppers, leaves = upper_mats.shape[0], leaf_mats.shape[0]
    entries, rank = places.shape[1], down.shape[2]
    members = replies[0].shape[0] // groups
    size = basis.shape[1] // leaves
    fan = entries // (uppers + leaves)
    parts = out_sems.shape[0]
    loads = [
        pltpu.make_async_copy(source, target, sems.at[i])
        for i, (source, target) in enumerate(zip(sources, targets))
    ]
    for load in loads:
        load.start()
    group = jnp.transpose(places[...].astype(F32))
    group, position = group[:, 0:1], group[:, 1:2]
    first = 0
    for number, reply in enumerate(replies):
        rows = reply.shape[1] // 2
        stride = (rows + 15) // 16 * 16
        lane = iota((entries, groups * stride), 1).astype(F32)
        inside = (position >= first) & (position < first + rows)
        wanted = jnp.where(inside, group * stride + position - first, -1.0)
        chosen = jnp.where(wanted == lane, 1.0, 0.0).astype(BF16)
        first += rows
        taken[...] = jnp.zeros(taken.shape, BF16)
        loads[number].wait()
        for m in range(2 * members):
            for g in range(groups):
                taken[m % 2, g * stride : g * stride + rows] = reply[
                    m // 2 * groups + g, m % 2 * rows : (m % 2 + 1) * rows
                ]
            block = dot(chosen, taken[m % 2, : groups * stride])
            block = block.reshape(uppers + leaves, fan, 4 * rank)
            block = jnp.concatenate([block[:, :, : 2 * rank], block[:, :, 2 * rank :]], axis=1)
            cut = slice(m * 2 * fan, (m + 1) * 2 * fan)
            if number == 0:
                held[:, cut] = block.astype(BF16)
            else:
                held[:, cut] += block.astype(BF16)
    loads = loads[len(replies) :]
    loads[0].wait()
    loads[1].wait()
    for j in range(uppers):
        upper = folded(dot(upper_mats[j], held[leaves + j]), rank).astype(BF16)
        handed[j] = dot(down[j], upper)
    loads[2].wait()
    locals_ = []
    for c in range(leaves):
        local = folded(dot(leaf_mats[c], held[c]), rank)
        locals_.append(local + handed[c // 4, c % 4 * rank : (c % 4 + 1) * rank])
    tall = jnp.transpose(jnp.concatenate(locals_, axis=0)).astype(BF16)
    loads[3].wait()
    loads[4].wait()
    stores = []
    for part in range(parts):
        begin = part * leaves // parts
        for c in range(begin, begin + leaves // parts):
            cut = slice(c * size, (c + 1) * size)
            far = dot(tall[:, c * rank : (c + 1) * rank], basis[:, cut])
            out_here[:, cut] = (far + near[c]).astype(BF16)
        cut = pl.ds(begin * size, leaves * size // parts)
        stores.append(
            pltpu.make_async_copy(out_here.at[:, cut], out_ref.at[:, cut], out_sems.at[part])
        )
        stores[-1].start()
    for store in stores:
        store.wait()


def final(groups, places, replies, upper_mats, down, leaf_mats, basis, near):
    uppers, rank = down.shape[0], down.shape[2]
    operands = (*replies, upper_mats, down, leaf_mats, basis, near)
    out = jax.ShapeDtypeStruct((near.shape[1], basis.shape[1]), BF16)
    parts = 4
    return pl.pallas_call(
        lambda *refs: final_kernel(groups, *refs),
        out_shape=out,
        in_specs=[VMEM] + [ANY] * len(operands),
        out_specs=ANY,
        scratch_shapes=[pltpu.VMEM(x.shape, x.dtype) for x in (*operands, out)]
        + [
            pltpu.VMEM((2, groups * 32, replies[0].shape[2]), BF16),
            pltpu.VMEM((uppers + leaf_mats.shape[0], upper_mats.shape[2], 2 * rank), BF16),
            pltpu.VMEM((uppers, 4 * rank, rank), F32),
            pltpu.SemaphoreType.DMA((len(operands),)),
            pltpu.SemaphoreType.DMA((parts,)),
        ],
        compiler_params=pltpu.CompilerParams(vmem_limit_bytes=ROOM),
        name="far",
    )(places, *operands)


def exchange(value, axes):
    return lax.all_to_all(value, axes, split_axis=0, concat_axis=0, tiled=True)


def body(
    density,
    points,
    weights,
    source_basis,
    target_basis,
    up_transfer,
    down_transfer,
    couple_leaf,
    couple_upper,
    owner_leaf,
    local_leaf,
    owner_upper,
    local_upper,
    near_list,
):
    devices = lax.axis_size(AXES)
    members, groups = lax.axis_size("gx"), lax.axis_size("gy")
    leaves, fan = owner_leaf.shape
    uppers = owner_upper.shape[0]
    vectors = density.shape[0]
    rank = source_basis.shape[0]
    half = rank // 2
    rows = leaves + uppers

    asks, places = pl.pallas_call(
        request_kernel,
        out_shape=(
            jax.ShapeDtypeStruct((groups, 8, 256), BF16),
            jax.ShapeDtypeStruct((8, rows * fan), jnp.int32),
        ),
        in_specs=[VMEM] * 4,
        out_specs=(VMEM, VMEM),
        name="requests",
    )(owner_leaf.T, local_leaf.T, owner_upper, local_upper)
    asked = exchange(asks, "gy")
    slices = pl.pallas_call(
        multipole_kernel,
        out_shape=jax.ShapeDtypeStruct((members, 2 * rows, 4 * rank), BF16),
        in_specs=[VMEM] * 3,
        out_specs=VMEM,
        scratch_shapes=[
            pltpu.VMEM((rows * rank, vectors), F32),
            pltpu.VMEM((rows * half, 2 * vectors), F32),
            pltpu.VMEM((leaves * half, 2 * rank), F32),
        ],
        compiler_params=pltpu.CompilerParams(vmem_limit_bytes=ROOM),
        name="multipoles",
    )(density, source_basis, up_transfer)

    slices, asked, density, points, weights = lax.optimization_barrier(
        (slices, asked, density, points, weights)
    )
    own = jnp.concatenate(
        [density, points, weights[None], jnp.zeros((4, density.shape[1]), BF16)], axis=0
    )
    one_side, other_side = swapped(own, 0), swapped(own, 1)
    asked = jnp.broadcast_to(asked[None, :, 0, :], (members, groups, asked.shape[2]))
    slices = jnp.concatenate([slices, asked], axis=1)

    slices, own, couple_leaf, couple_upper, down_transfer = lax.optimization_barrier(
        (slices, own, couple_leaf, couple_upper, down_transfer)
    )
    slices = exchange(slices, "gx")
    upper_mats = arrange(couple_upper)
    leaf_mats = arrange(couple_leaf)
    down = (
        down_transfer.reshape(uppers, 4, rank, rank)
        .transpose(0, 1, 3, 2)
        .reshape(uppers, 4 * rank, rank)
    )
    place = lax.axis_index(AXES)
    first = jnp.stack([place * leaves, jnp.int32(leaves * devices), place % 2])
    slices, leaf_mats, upper_mats, down, first = lax.optimization_barrier(
        (slices, leaf_mats, upper_mats, down, first)
    )
    replies = exchange(serve(slices, groups, 0, 2 * SENT), AXES)
    near = near_field(near_list.T, first, one_side, own, other_side, leaves, vectors)
    near, late = lax.optimization_barrier((near, slices[:, 2 * rows :]))
    most = jnp.max(late[:, :, 127].astype(F32))

    def finish(*received):
        return final(groups, places, received, upper_mats, down, leaf_mats, target_basis, near)

    def some_left():
        others = exchange(serve(slices, groups, 2 * SENT, 2 * (MOST - SENT)), AXES)
        return finish(replies, others)

    return lax.cond(most > SENT, some_left, lambda: finish(replies))


def solution(mesh):
    whole = AXES
    placed = (
        P(None, whole),
        P(None, whole),
        P(whole),
        P(None, whole),
        P(None, whole),
        P(whole, None),
        P(whole, None),
        P(whole, None, None),
        P(whole, None, None),
        P(whole, None),
        P(whole, None),
        P(whole, None),
        P(whole, None),
        P(whole, None),
    )
    return jax.shard_map(
        body, mesh=mesh, in_specs=placed, out_specs=P(None, whole), check_vma=False
    )
```

```python
import jax
import jax.numpy as jnp
from jax import lax
from jax.experimental import pallas as pl
from jax.experimental.pallas import tpu as pltpu
from jax.sharding import PartitionSpec as P

SOFTEN = 0.0025
AXES = ("gx", "gy")
SENT = 28
MOST = 40
F32 = jnp.float32
BF16 = jnp.bfloat16
NN = (((1,), (0,)), ((), ()))
NT = (((1,), (1,)), ((), ()))
TN = (((0,), (0,)), ((), ()))
VMEM = pl.BlockSpec(memory_space=pltpu.VMEM)
ANY = pl.BlockSpec(memory_space=pl.ANY)
ROOM = 60 << 20
SMEM = pl.BlockSpec(memory_space=pltpu.SMEM)


def dot(a, b, dims=NN):
    return lax.dot_general(a, b, dims, preferred_element_type=F32)


def swapped(value, first):
    count = lax.axis_size(AXES)
    pairs = [(one, (one + 1) % count) for one in range(first, count, 2)]
    return lax.ppermute(value, AXES, pairs + [(b, a) for a, b in pairs])


def iota(shape, dim):
    return lax.broadcasted_iota(jnp.int32, shape, dim)


def folded(pair, rank):
    return pair[:rank, :rank] + pair[rank:, rank:]


def flat_row(table):
    wide, rows = table.shape
    spread = (iota((rows, rows * wide), 1) // wide == iota((rows, rows * wide), 0)).astype(BF16)
    keep = iota((wide, rows * wide), 1) % wide == iota((wide, rows * wide), 0)
    return jnp.sum(
        jnp.where(keep, dot(table.astype(F32).astype(BF16), spread), 0.0), axis=0, keepdims=True
    ).astype(jnp.int32)


def request_kernel(own_leaf, loc_leaf, own_upper, loc_upper, ask_ref, place_ref):
    groups = ask_ref.shape[0]
    leaves, uppers = own_leaf.shape[1], own_upper.shape[0]
    tall_owner, tall_row = jnp.transpose(own_upper[...]), jnp.transpose(loc_upper[...])
    owner = jnp.concatenate([flat_row(own_leaf[...]), flat_row(tall_owner)], axis=1)
    row = jnp.concatenate([flat_row(loc_leaf[...]), flat_row(tall_row) + leaves], axis=1)
    entries = owner.shape[1]
    member = owner // groups
    group = owner - member * groups
    hit = group == iota((groups, entries), 0)
    ones = hit.astype(BF16)
    before = (iota((entries, entries), 0) < iota((entries, entries), 1)).astype(BF16)
    rank = jnp.sum(jnp.where(hit, dot(ones, before), 0.0), axis=0, keepdims=True).astype(jnp.int32)
    slot = jnp.where(rank < SENT, rank, rank + SENT)
    second = slot + jnp.where(rank < SENT, SENT, MOST - SENT)
    first_here = slot == iota((128, entries), 0)
    second_here = second == iota((128, entries), 0)
    far_row = row + (leaves + uppers)
    members = jnp.where(first_here | second_here, member, 0)
    rows = jnp.where(first_here, row, jnp.where(second_here, far_row, 0))
    wanted = [dot(ones, part.astype(F32).astype(BF16), NT) for part in (members, rows)]
    most = jnp.max(jnp.sum(hit.astype(F32), axis=1, keepdims=True), axis=0, keepdims=True)
    wanted[0] = jnp.where(iota((groups, 128), 1) == 127, most, wanted[0])
    both = jnp.concatenate(wanted, axis=1)
    for g in range(groups):
        ask_ref[g] = jnp.broadcast_to(both[g : g + 1], ask_ref.shape[1:]).astype(BF16)
    place_ref[...] = jnp.where(iota(place_ref.shape, 0) == 0, group, rank)


def multipole_kernel(density, basis, up_ref, out_ref, square, table, up):
    leaves = up_ref.shape[0]
    rank = square.shape[1]
    half = rank // 2
    rows = out_ref.shape[1] // 2
    size = density.shape[1] // leaves
    for leaf in range(leaves):
        cut = slice(leaf * size, (leaf + 1) * size)
        square[leaf * rank : (leaf + 1) * rank] = dot(basis[:, cut], density[:, cut], NT)

    def pack(first, count):
        even = square[pl.ds(first * rank, count * half, stride=2)]
        odd = square[pl.ds(first * rank + 1, count * half, stride=2)]
        table[first * half : (first + count) * half] = jnp.concatenate([even, odd], axis=1)

    pack(0, leaves)
    for j in range(half):
        up[pl.ds(j, leaves, stride=half)] = up_ref[:, j * 2 * rank : (j + 1) * 2 * rank].astype(F32)
    for upper in range(rows - leaves):
        cut = slice(upper * 4 * half, (upper + 1) * 4 * half)
        pair = dot(up[cut].astype(BF16), table[cut].astype(BF16), TN)
        square[(leaves + upper) * rank : (leaves + upper + 1) * rank] = folded(pair, rank)
    pack(leaves, rows - leaves)
    for m in range(out_ref.shape[0]):
        parts = [table[pl.ds(4 * m + a, rows, stride=half)] for a in range(4)]
        pairs = [jnp.concatenate(parts[:2], axis=1), jnp.concatenate(parts[2:], axis=1)]
        out_ref[m] = jnp.concatenate(pairs, axis=0).astype(BF16)


def serve_kernel(first, slices, out_ref, codes):
    step = pl.program_id(0)
    members, count, wide = slices.shape
    rows = out_ref.shape[1]
    asking = codes.shape[2]
    some = out_ref.shape[0] // asking

    @pl.when(step == 0)
    def _():
        asked = slices[:, count - asking :, :].astype(F32)
        code = asked[:, :, : wide // 2] * count + asked[:, :, wide // 2 :]
        for m in range(members):
            codes[m] = jnp.transpose(code[m])

    lanes = iota((rows, members * count), 1).astype(F32)
    table = slices[...].reshape(members * count, wide)
    for m in range(some):
        column = codes[step * some + m, first : first + rows]
        for t in range(0, asking, 4):
            picks = jnp.concatenate(
                [jnp.where(column[:, u : u + 1] == lanes, 1.0, 0.0) for u in range(t, t + 4)],
                axis=0,
            ).astype(BF16)
            out_ref[m * asking + t : m * asking + t + 4] = (
                dot(picks, table).reshape(4, rows, wide).astype(BF16)
            )


def serve(slices, asking, first, rows):
    members, count, wide = slices.shape
    some = members // 2
    return pl.pallas_call(
        lambda *refs: serve_kernel(first, *refs),
        out_shape=jax.ShapeDtypeStruct((members * asking, rows, wide), BF16),
        grid=(members // some,),
        in_specs=[pl.BlockSpec(slices.shape, lambda i: (0, 0, 0))],
        out_specs=pl.BlockSpec((some * asking, rows, wide), lambda i: (i, 0, 0)),
        scratch_shapes=[pltpu.VMEM((members, wide // 2, asking), F32)],
        compiler_params=pltpu.CompilerParams(vmem_limit_bytes=ROOM),
        name="serve",
    )(slices)


def arrange_kernel(couple, out_ref):
    for c in range(couple.shape[0]):
        mats = couple[c].astype(F32)
        tall = jnp.concatenate(
            [mats[:, j * 128 : (j + 1) * 128] for j in range(mats.shape[1] // 128)], axis=0
        )
        out_ref[c] = jnp.transpose(tall).astype(BF16)


def arrange(couple):
    count, fan, wide = couple.shape
    per_step = 8
    return pl.pallas_call(
        arrange_kernel,
        out_shape=jax.ShapeDtypeStruct((count, 128, wide * fan // 128), BF16),
        grid=(count // per_step,),
        in_specs=[pl.BlockSpec((per_step, fan, wide), lambda i: (i, 0, 0))],
        out_specs=pl.BlockSpec((per_step, 128, wide * fan // 128), lambda i: (i, 0, 0)),
        compiler_params=pltpu.CompilerParams(vmem_limit_bytes=ROOM),
        name="arrange",
    )(couple)


def pieces(value):
    high = value.astype(BF16).astype(F32)
    middle = (value - high).astype(BF16).astype(F32)
    return high, middle, value - high - middle


def near_kernel(listed, first, one_side, own, other_side, out_ref, window, sources, targets, kern):
    leaves, rows, size = out_ref.shape
    near = listed.shape[0]
    wide = own.shape[1]
    total = first[1]
    one = jnp.ones((3, wide), F32)
    zero = jnp.zeros((6, wide), F32)
    odd = first[2]
    for ref, place in ((one_side, 2 - 2 * odd), (own, 1), (other_side, 2 * odd)):
        cut = pl.ds(pl.multiple_of(place * wide, wide), wide)
        window[:, cut] = ref[:rows]
        y = ref[rows:].astype(F32)
        square = y[0:1] * y[0:1] + y[1:2] * y[1:2] + y[2:3] * y[2:3]
        sources[cut] = jnp.transpose(
            jnp.concatenate([-2.0 * y[0:3], one, *pieces(square + SOFTEN), y[3:4], zero], axis=0)
        ).astype(BF16)
        if ref is own:
            targets[...] = jnp.concatenate(
                [y[0:3], *pieces(square), one, zero, zero[:1]], axis=0
            ).astype(BF16)

    def span(leaf):
        return pl.ds(pl.multiple_of(leaf * size, size), size)

    def place_of(c, k):
        offset = listed[k, c] - first[0] + leaves
        offset = jnp.where(offset < 0, offset + total, offset)
        return span(jnp.where(offset >= total, offset - total, offset))

    def fill(c, k, slot):
        block = sources[place_of(c, k)]
        square = dot(block, targets[:, span(c)])
        kern[slot, k] = (block[:, 9:10].astype(F32) * lax.rsqrt(square)).astype(BF16)

    def both(filled, used, slot):
        sum_ = jnp.zeros((rows, size), F32)
        for k in range(near):
            fill(filled, k, 1 - slot)
            sum_ += dot(window[:, place_of(used, k)], kern[slot, k])
        out_ref[used] = sum_

    for k in range(near):
        fill(0, k, 0)

    def two(i, carry):
        both(2 * i + 1, 2 * i, 0)
        both(jnp.minimum(2 * i + 2, leaves - 1), 2 * i + 1, 1)
        return carry

    lax.fori_loop(0, leaves // 2, two, 0)


def near_field(listed, first, one_side, own, other_side, leaves, rows):
    wide = own.shape[1]
    size = wide // leaves
    near = listed.shape[0]
    return pl.pallas_call(
        near_kernel,
        out_shape=jax.ShapeDtypeStruct((leaves, rows, size), F32),
        in_specs=[SMEM, SMEM, VMEM, VMEM, VMEM],
        out_specs=VMEM,
        scratch_shapes=[
            pltpu.VMEM((rows, 3 * wide), BF16),
            pltpu.VMEM((3 * wide, 16), BF16),
            pltpu.VMEM((16, wide), BF16),
            pltpu.VMEM((2, near, size, size), BF16),
        ],
        compiler_params=pltpu.CompilerParams(vmem_limit_bytes=ROOM),
        cost_estimate=pl.CostEstimate(
            flops=400 * leaves * near * size * size * rows,
            bytes_accessed=6 << 20,
            transcendentals=leaves * near * size * size,
        ),
        name="near",
    )(listed, first, one_side, own, other_side)


def final_kernel(groups, places, *refs):
    count = (len(refs) - 5) // 2
    sources, out_ref, refs = refs[: count - 1], refs[count - 1], refs[count:]
    targets, out_here, (taken, held, handed, sems, out_sems) = (
        refs[: count - 1],
        refs[count - 1],
        refs[count:],
    )
    replies = targets[:-5]
    upper_mats, down, leaf_mats, basis, near = targets[-5:]
    uppers, leaves = upper_mats.shape[0], leaf_mats.shape[0]
    entries, rank = places.shape[1], down.shape[2]
    members = replies[0].shape[0] // groups
    size = basis.shape[1] // leaves
    fan = entries // (uppers + leaves)
    parts = out_sems.shape[0]
    loads = [
        pltpu.make_async_copy(source, target, sems.at[i])
        for i, (source, target) in enumerate(zip(sources, targets))
    ]
    for load in loads:
        load.start()
    group = jnp.transpose(places[...].astype(F32))
    group, position = group[:, 0:1], group[:, 1:2]
    first = 0
    for number, reply in enumerate(replies):
        rows = reply.shape[1] // 2
        stride = (rows + 15) // 16 * 16
        lane = iota((entries, groups * stride), 1).astype(F32)
        inside = (position >= first) & (position < first + rows)
        wanted = jnp.where(inside, group * stride + position - first, -1.0)
        chosen = jnp.where(wanted == lane, 1.0, 0.0).astype(BF16)
        first += rows
        taken[...] = jnp.zeros(taken.shape, BF16)
        loads[number].wait()
        for m in range(2 * members):
            for g in range(groups):
                taken[m % 2, g * stride : g * stride + rows] = reply[
                    m // 2 * groups + g, m % 2 * rows : (m % 2 + 1) * rows
                ]
            block = dot(chosen, taken[m % 2, : groups * stride])
            block = block.reshape(uppers + leaves, fan, 4 * rank)
            block = jnp.concatenate([block[:, :, : 2 * rank], block[:, :, 2 * rank :]], axis=1)
            cut = slice(m * 2 * fan, (m + 1) * 2 * fan)
            if number == 0:
                held[:, cut] = block.astype(BF16)
            else:
                held[:, cut] += block.astype(BF16)
    loads = loads[len(replies) :]
    loads[0].wait()
    loads[1].wait()
    for j in range(uppers):
        upper = folded(dot(upper_mats[j], held[leaves + j]), rank).astype(BF16)
        handed[j] = dot(down[j], upper)
    loads[2].wait()
    locals_ = []
    for c in range(leaves):
        local = folded(dot(leaf_mats[c], held[c]), rank)
        locals_.append(local + handed[c // 4, c % 4 * rank : (c % 4 + 1) * rank])
    tall = jnp.transpose(jnp.concatenate(locals_, axis=0)).astype(BF16)
    loads[3].wait()
    loads[4].wait()
    stores = []
    for part in range(parts):
        begin = part * leaves // parts
        for c in range(begin, begin + leaves // parts):
            cut = slice(c * size, (c + 1) * size)
            far = dot(tall[:, c * rank : (c + 1) * rank], basis[:, cut])
            out_here[:, cut] = (far + near[c]).astype(BF16)
        cut = pl.ds(begin * size, leaves * size // parts)
        stores.append(
            pltpu.make_async_copy(out_here.at[:, cut], out_ref.at[:, cut], out_sems.at[part])
        )
        stores[-1].start()
    for store in stores:
        store.wait()


def final(groups, places, replies, upper_mats, down, leaf_mats, basis, near):
    uppers, rank = down.shape[0], down.shape[2]
    operands = (*replies, upper_mats, down, leaf_mats, basis, near)
    out = jax.ShapeDtypeStruct((near.shape[1], basis.shape[1]), BF16)
    parts = 4
    return pl.pallas_call(
        lambda *refs: final_kernel(groups, *refs),
        out_shape=out,
        in_specs=[VMEM] + [ANY] * len(operands),
        out_specs=ANY,
        scratch_shapes=[pltpu.VMEM(x.shape, x.dtype) for x in (*operands, out)]
        + [
            pltpu.VMEM((2, groups * 32, replies[0].shape[2]), BF16),
            pltpu.VMEM((uppers + leaf_mats.shape[0], upper_mats.shape[2], 2 * rank), BF16),
            pltpu.VMEM((uppers, 4 * rank, rank), F32),
            pltpu.SemaphoreType.DMA((len(operands),)),
            pltpu.SemaphoreType.DMA((parts,)),
        ],
        compiler_params=pltpu.CompilerParams(vmem_limit_bytes=ROOM),
        name="far",
    )(places, *operands)


def exchange(value, axes):
    return lax.all_to_all(value, axes, split_axis=0, concat_axis=0, tiled=True)


def body(
    density,
    points,
    weights,
    source_basis,
    target_basis,
    up_transfer,
    down_transfer,
    couple_leaf,
    couple_upper,
    owner_leaf,
    local_leaf,
    owner_upper,
    local_upper,
    near_list,
):
    devices = lax.axis_size(AXES)
    members, groups = lax.axis_size("gx"), lax.axis_size("gy")
    leaves, fan = owner_leaf.shape
    uppers = owner_upper.shape[0]
    vectors = density.shape[0]
    rank = source_basis.shape[0]
    half = rank // 2
    rows = leaves + uppers

    asks, places = pl.pallas_call(
        request_kernel,
        out_shape=(
            jax.ShapeDtypeStruct((groups, 8, 256), BF16),
            jax.ShapeDtypeStruct((8, rows * fan), jnp.int32),
        ),
        in_specs=[VMEM] * 4,
        out_specs=(VMEM, VMEM),
        name="requests",
    )(owner_leaf.T, local_leaf.T, owner_upper, local_upper)
    asked = exchange(asks, "gy")
    slices = pl.pallas_call(
        multipole_kernel,
        out_shape=jax.ShapeDtypeStruct((members, 2 * rows, 4 * rank), BF16),
        in_specs=[VMEM] * 3,
        out_specs=VMEM,
        scratch_shapes=[
            pltpu.VMEM((rows * rank + 8, vectors), F32),
            pltpu.VMEM((rows * half + half, 2 * vectors), F32),
            pltpu.VMEM((leaves * half + half, 2 * rank), F32),
        ],
        compiler_params=pltpu.CompilerParams(vmem_limit_bytes=ROOM),
        name="multipoles",
    )(density, source_basis, up_transfer)

    slices, asked, density, points, weights = lax.optimization_barrier(
        (slices, asked, density, points, weights)
    )
    own = jnp.concatenate(
        [density, points, weights[None], jnp.zeros((4, density.shape[1]), BF16)], axis=0
    )
    one_side, other_side = swapped(own, 0), swapped(own, 1)
    asked = jnp.broadcast_to(asked[None, :, 0, :], (members, groups, asked.shape[2]))
    slices = jnp.concatenate([slices, asked], axis=1)

    slices, own, couple_leaf, couple_upper, down_transfer = lax.optimization_barrier(
        (slices, own, couple_leaf, couple_upper, down_transfer)
    )
    slices = exchange(slices, "gx")
    upper_mats = arrange(couple_upper)
    leaf_mats = arrange(couple_leaf)
    down = (
        down_transfer.reshape(uppers, 4, rank, rank)
        .transpose(0, 1, 3, 2)
        .reshape(uppers, 4 * rank, rank)
    )
    place = lax.axis_index(AXES)
    first = jnp.stack([place * leaves, jnp.int32(leaves * devices), place % 2])
    slices, leaf_mats, upper_mats, down, first = lax.optimization_barrier(
        (slices, leaf_mats, upper_mats, down, first)
    )
    replies = exchange(serve(slices, groups, 0, 2 * SENT), AXES)
    near = near_field(near_list.T, first, one_side, own, other_side, leaves, vectors)
    near, late = lax.optimization_barrier((near, slices[:, 2 * rows :]))
    most = jnp.max(late[:, :, 127].astype(F32))

    def finish(*received):
        return final(groups, places, received, upper_mats, down, leaf_mats, target_basis, near)

    def some_left():
        others = exchange(serve(slices, groups, 2 * SENT, 2 * (MOST - SENT)), AXES)
        return finish(replies, others)

    return lax.cond(most > SENT, some_left, lambda: finish(replies))


def solution(mesh):
    whole = AXES
    placed = (
        P(None, whole),
        P(None, whole),
        P(whole),
        P(None, whole),
        P(None, whole),
        P(whole, None),
        P(whole, None),
        P(whole, None, None),
        P(whole, None, None),
        P(whole, None),
        P(whole, None),
        P(whole, None),
        P(whole, None),
        P(whole, None),
    )
    return jax.shard_map(
        body, mesh=mesh, in_specs=placed, out_specs=P(None, whole), check_vma=False
    )
```
